512 devices in a mesh: cp: 32 (over z, core), hd: 4 (over x), dp: 4 (over y).
Axes of the slice: x: 4, y: 4, z: 16, core: 2. Of those that a mesh axis runs over, the one named last changes fastest.
Arguments:
- queries: bfloat16 [32768, 4096], P(('dp', 'cp'), 'hd'), parts along dimension 0, may hold values from -10 to 10
- keys: bfloat16 [32768, 512], P(('dp', 'cp'), 'hd'), parts along dimension 0, may hold values from -4.5 to 4.5
- values: bfloat16 [32768, 512], P(('dp', 'cp'), 'hd'), parts along dimension 0, may hold values from -6 to 6
- outputs: bfloat16 [32768, 4096], P(('dp', 'cp'), 'hd'), parts along dimension 0, may hold values from -6 to 6
- out_grad: bfloat16 [32768, 4096], P(('dp', 'cp'), 'hd'), parts along dimension 0, may hold values from -6 to 6
- doc_lengths: int32 [204], P('dp'), parts along dimension 0, may hold values from 1 to 1920, as said below
- block_offsets: int32 [128, 16], P(('dp', 'cp')), parts along dimension 0, may hold values from -1 to 7, as said below
Outputs:
- grad_queries: bfloat16 [32768, 4096], P(('dp', 'cp'), 'hd'), parts along dimension 0
- grad_keys: bfloat16 [32768, 512], P(('dp', 'cp'), 'hd'), parts along dimension 0
- grad_values: bfloat16 [32768, 512], P(('dp', 'cp'), 'hd'), parts along dimension 0
The draws below stay inside these ranges and needn't reach their ends.
There are 4 independent parts, one for each index of `dp`. The reference program is written for one: setup_inputs(seed, part) draws one part's arguments, and reference() takes and returns one part's arrays. A program takes and returns all parts, laid end to end along the dimension named above; each array names one. Nothing has to cross between parts.
Inputs may be any that keep to these rules, and one draw needn't show every extreme that they name: `doc_lengths`: documents are whole numbers of tokens in order that sum to 8192; the longest holds exactly 1920 tokens. `block_offsets`: row b holds each of the offsets 0, 1, ..., m_b exactly once, in slots and an order drawn from the seed, and -1 in its other slots, where j <= m_b exactly when some token of block b - j shares a document with some token of block b at or before it; some row holds 7.
All inputs are finite; a program needn't handle non-finite values.
Results may differ from the reference program's by a relative error of at most 0.0049.
Values may be sent and summed in bfloat16 or wider, within the bound.
No kernel may reach another device: no remote copies, remote signals or barrier semaphores. Data moves between devices by JAX's collectives and lax.ppermute only.
A program may use at most 64 MiB of HBM per device.

```python
import jax
import jax.numpy as jnp
from jax import lax

HQ = 32
KVH = 4
HD = 128
TOK_DEV = 256
SPAN = 8
TOKENS = 8192
DOCS = 51
N_CP = 32


def doc_layout(key):
    unit = TOK_DEV // 2
    unit_count = 2 * N_CP
    longest = SPAN * TOK_DEV - unit
    start_block = jax.random.randint(jax.random.fold_in(key, 11), (), 0, N_CP - SPAN + 1)
    inner = jax.random.randint(jax.random.fold_in(key, 12), (), 1, unit)
    jitter = jax.random.randint(jax.random.fold_in(key, 13), (unit_count + 1,), 0, unit)
    grid_ids = jnp.arange(unit_count + 1, dtype=jnp.int32)
    low_id = 2 * start_block
    high_id = low_id + 2 * SPAN
    pinned = (grid_ids == 0) | (grid_ids == unit_count) | (grid_ids == low_id) | (grid_ids == high_id)
    marks = grid_ids * unit + jnp.where(pinned, 0, jitter)
    inside = (grid_ids > low_id) & (grid_ids < high_id)
    marks = jnp.where(inside, 2 * TOKENS + grid_ids, marks)
    heavy_start = low_id * unit + inner
    all_marks = jnp.concatenate([marks, jnp.stack([heavy_start, heavy_start + longest])])
    ordered = jnp.sort(all_marks)[:DOCS + 1]
    return (ordered[1:] - ordered[:-1]).astype(jnp.int32)


def shared_keys(key):
    return jax.random.normal(jax.random.fold_in(key, 21), (TOKENS, KVH * HD), jnp.float32)


def draw_doc_lengths(key, part):
    lengths = doc_layout(key)
    return lengths


def draw_block_offsets(key, part):
    lengths = doc_layout(key)
    key = jax.random.fold_in(key, 2)
    doc_ends = jnp.cumsum(lengths)
    block_ids = jnp.arange(N_CP, dtype=jnp.int32)
    first_seg = jnp.sum((block_ids[:, None] * TOK_DEV >= doc_ends[None, :]).astype(jnp.int32), axis=1)
    last_seg = jnp.sum((block_ids[:, None] * TOK_DEV + TOK_DEV - 1 >= doc_ends[None, :]).astype(jnp.int32), axis=1)
    offsets = jnp.arange(SPAN, dtype=jnp.int32)
    earlier = block_ids[:, None] - offsets[None, :]
    present = (earlier >= 0) & (first_seg[:, None] <= last_seg[jnp.clip(earlier, 0, N_CP - 1)])
    listed = jnp.where(present, offsets[None, :], -1).astype(jnp.int32)
    slots = jnp.concatenate([listed, jnp.full((N_CP, SPAN), -1, jnp.int32)], axis=1)
    slot_ids = jnp.arange(2 * SPAN, dtype=jnp.int32)
    scores = jax.random.randint(key, (N_CP, 2 * SPAN), 0, 1 << 20) * (2 * SPAN) + slot_ids[None, :]
    order = jnp.argsort(scores, axis=1, stable=True)
    return jnp.take_along_axis(slots, order, axis=1).astype(jnp.int32)


def draw_keys(key, part):
    base_keys = shared_keys(key)
    clipped = jnp.clip(base_keys, -4.5, 4.5)
    result = clipped
    return result.astype(jnp.bfloat16)


def draw_queries(key, part):
    key = jax.random.fold_in(key, 4)
    fresh_draw = jnp.clip(jax.random.normal(key, (TOKENS, HQ * HD), jnp.float32), -4.5, 4.5)
    result = fresh_draw
    return result.astype(jnp.bfloat16)


def block_levels(key, extent, split, smallest, high):
    loudness, own = 1.0, jax.random.fold_in(key, 6)
    for position, shards_of in split:
        steps = jnp.exp(jax.random.uniform(jax.random.fold_in(own, position), (shards_of,), jnp.float32, smallest / len(split), high / len(split)))
        loudness = loudness * jnp.repeat(steps, extent[position] // shards_of).reshape([-1 if axis == position else 1 for axis in range(len(extent))])
    return loudness


def gaussian(rng, dims, spread, bound, shards=(), kind=jnp.bfloat16):
    drawn = spread * jax.random.normal(rng, dims, jnp.float32)
    if shards:
        drawn = drawn * block_levels(rng, dims, shards, -0.22, 0.18)
    return jnp.clip(drawn, -bound, bound).astype(kind)


def setup_inputs(seed: int = 0, part: int = 0) -> dict:
    streams_of = jax.random.split(jax.random.key(seed), 8)
    part_splits = jax.random.split(jax.random.fold_in(streams_of[7], part), 8)
    return {
        "queries": draw_queries(jax.random.fold_in(jax.random.fold_in(streams_of[7], part), 71), part),
        "keys": draw_keys(jax.random.fold_in(jax.random.fold_in(streams_of[7], part), 71), part),
        "values": gaussian(part_splits[2], (TOKENS, KVH * HD), 1.0, 6.0, ((0, 32), (1, 4))),
        "outputs": gaussian(part_splits[3], (TOKENS, HQ * HD), 1.0, 6.0, ((0, 32), (1, 4))),
        "out_grad": gaussian(part_splits[4], (TOKENS, HQ * HD), 1.0, 6.0, ((0, 32), (1, 4))),
        "doc_lengths": draw_doc_lengths(jax.random.fold_in(jax.random.fold_in(streams_of[7], part), 71), part),
        "block_offsets": draw_block_offsets(jax.random.fold_in(jax.random.fold_in(streams_of[7], part), 71), part),
    }


NEG_FILL = -1.0e30


def segment_of(positions, doc_ends):
    return jnp.sum((positions[:, None] >= doc_ends[None, :]).astype(jnp.int32), axis=1)


def reference(queries, keys, values, outputs, out_grad, doc_lengths, block_offsets):
    group_size = HQ // KVH
    factor = HD ** -0.5
    margin = (SPAN - 1) * TOK_DEV
    width_rows = SPAN * TOK_DEV
    doc_ends = jnp.cumsum(doc_lengths).astype(jnp.int32)
    key_pad = jnp.concatenate([jnp.zeros((margin, KVH * HD), keys.dtype), keys], axis=0)
    value_pad = jnp.concatenate([jnp.zeros((margin, KVH * HD), values.dtype), values], axis=0)
    delta_all = jnp.sum((out_grad.astype(jnp.float32) * outputs.astype(jnp.float32)).reshape(TOKENS, KVH, group_size, HD), axis=3)
    q_rows = jnp.arange(TOK_DEV, dtype=jnp.int32)
    w_rows = jnp.arange(width_rows, dtype=jnp.int32)
    window_offset = (SPAN - 1 - w_rows // TOK_DEV).astype(jnp.int32)

    def visit_block(block_idx, carried):
        grad_q, grad_k, grad_v = carried
        block_idx = jnp.asarray(block_idx).astype(jnp.int32)
        row_start = (block_idx * TOK_DEV).astype(jnp.int32)
        q_block = lax.dynamic_slice_in_dim(queries, row_start, TOK_DEV, 0).astype(jnp.float32).reshape(TOK_DEV, KVH, group_size, HD)
        g_block = lax.dynamic_slice_in_dim(out_grad, row_start, TOK_DEV, 0).astype(jnp.float32).reshape(TOK_DEV, KVH, group_size, HD)
        delta_rows = jnp.transpose(lax.dynamic_slice_in_dim(delta_all, row_start, TOK_DEV, 0), (1, 2, 0))
        k_win = lax.dynamic_slice_in_dim(key_pad, row_start, width_rows, 0).astype(jnp.float32).reshape(width_rows, KVH, HD)
        v_win = lax.dynamic_slice_in_dim(value_pad, row_start, width_rows, 0).astype(jnp.float32).reshape(width_rows, KVH, HD)
        q_pos = row_start + q_rows
        k_pos = row_start - margin + w_rows
        listed_row = lax.dynamic_index_in_dim(block_offsets, block_idx, 0, keepdims=False)
        listed = jnp.any(listed_row[None, :] == window_offset[:, None], axis=1)
        pair_mask = (segment_of(q_pos, doc_ends)[:, None] == segment_of(k_pos, doc_ends)[None, :])
        pair_mask = pair_mask & (k_pos[None, :] <= q_pos[:, None]) & (k_pos[None, :] >= 0) & listed[None, :]
        scores = factor * jnp.einsum("tkgd,ukd->kgtu", q_block, k_win)
        masked = jnp.where(pair_mask, scores, NEG_FILL)
        row_max = jnp.max(masked, axis=3)
        summed = jnp.sum(jnp.where(pair_mask, jnp.exp(masked - row_max[..., None]), 0.0), axis=3)
        lse = row_max + jnp.log(summed)
        probs = jnp.where(pair_mask, jnp.exp(scores - lse[..., None]), 0.0)
        probs_low = lax.optimization_barrier(probs.astype(jnp.bfloat16)).astype(jnp.float32)
        d_prob = jnp.einsum("tkgd,ukd->kgtu", g_block, v_win)
        d_score = lax.optimization_barrier((probs * (d_prob - delta_rows[..., None])).astype(jnp.bfloat16)).astype(jnp.float32)
        grad_rows = (factor * jnp.einsum("kgtu,ukd->tkgd", d_score, k_win)).reshape(TOK_DEV, HQ * HD).astype(jnp.bfloat16)
        d_key = (factor * jnp.einsum("kgtu,tkgd->ukd", d_score, q_block)).reshape(width_rows, KVH * HD)
        d_value = jnp.einsum("kgtu,tkgd->ukd", probs_low, g_block).reshape(width_rows, KVH * HD)
        grad_q = lax.dynamic_update_slice_in_dim(grad_q, grad_rows, row_start, 0)
        grad_k = lax.dynamic_update_slice_in_dim(grad_k, lax.dynamic_slice_in_dim(grad_k, row_start, width_rows, 0) + d_key, row_start, 0)
        grad_v = lax.dynamic_update_slice_in_dim(grad_v, lax.dynamic_slice_in_dim(grad_v, row_start, width_rows, 0) + d_value, row_start, 0)
        return grad_q, grad_k, grad_v

    initial = (jnp.zeros((TOKENS, HQ * HD), jnp.bfloat16),
               jnp.zeros((TOKENS + margin, KVH * HD), jnp.float32),
               jnp.zeros((TOKENS + margin, KVH * HD), jnp.float32))
    grad_q, grad_k, grad_v = lax.fori_loop(0, TOKENS // TOK_DEV, visit_block, initial)
    return grad_q, grad_k[margin:].astype(jnp.bfloat16), grad_v[margin:].astype(jnp.bfloat16)
```

```python
import functools

import jax
import jax.numpy as jnp
from jax import lax
from jax.experimental import pallas as pl
from jax.experimental.pallas import tpu as pltpu
from jax.sharding import PartitionSpec as P

HD = 128
FACTOR = HD ** (-0.5)
SCORE_SCALE = FACTOR * 1.4426950408889634
MASKED = -1e30
EMPTY = -1e20
VMEM_BYTES = 32 * 1024 * 1024


def shift(array, by, parity=None):
    n = lax.axis_size("cp")
    pairs = [(i, (i + by) % n) for i in range(n) if parity is None or i % 2 == parity]
    return lax.ppermute(array, "cp", pairs)


def exchange(array):
    n = lax.axis_size("cp")
    return lax.ppermute(array, "cp", [(i, i ^ 1) for i in range(n)])


def nt_dot(a, b):
    return lax.dot_general(a, b, (((1,), (1,)), ((), ())), preferred_element_type=jnp.float32)


def nn_dot(a, b):
    return lax.dot_general(a, b, (((1,), (0,)), ((), ())), preferred_element_type=jnp.float32)


def side_block(side):
    block = lax.axis_index("cp")
    if side == 0:
        return block
    return block + 1 - 2 * lax.rem(block, 2)


def listed_pair(pay_ref, rows, side, slot):
    key_block = lax.axis_index("cp") - 2 * slot
    offset = side_block(side) - key_block
    row = pay_ref[rows:, 0:HD].astype(jnp.float32)
    hits = jnp.max((row == offset.astype(jnp.float32)).astype(jnp.float32))
    return (hits > 0.0) & (offset >= 0) & (key_block >= 0)


def write_bias(bias_ref, start_ref, side, slot):
    rows = bias_ref.shape[0]
    key_pos = (lax.axis_index("cp") - 2 * slot) * rows + lax.broadcasted_iota(jnp.int32, bias_ref.shape, 0)
    q_pos = side_block(side) * rows + lax.broadcasted_iota(jnp.int32, bias_ref.shape, 1)
    allowed = (key_pos >= start_ref[side : side + 1, :]) & (key_pos <= q_pos)
    bias_ref[...] = jnp.where(allowed, 0.0, MASKED)


def head_cols(head):
    return pl.ds(pl.multiple_of(head * HD, HD), HD)


def prep_kernel(q_ref, g_ref, o_ref, off_ref, pay_ref, delta_ref):
    rows, width = q_ref.shape
    slots = off_ref.shape[1]
    pay_ref[0:rows, 0:width] = q_ref[...]
    pay_ref[0:rows, width:] = g_ref[...]
    pay_ref[rows:, :] = jnp.full((16, 2 * width), -1.0, jnp.bfloat16)
    listed = jnp.broadcast_to(off_ref[...].astype(jnp.float32), (16, slots))
    pay_ref[rows:, 0:slots] = listed.astype(jnp.bfloat16)
    for head in range(width // HD):
        cols = slice(head * HD, (head + 1) * HD)
        product = g_ref[:, cols].astype(jnp.float32) * o_ref[:, cols].astype(jnp.float32)
        delta_ref[head : head + 1, :] = jnp.sum(product.T, axis=0, keepdims=True)


def stats_slots(slots, kv_refs, pay_refs, start_ref, m_ref, l_ref, bias_ref):
    rows = bias_ref.shape[0]
    heads = m_ref.shape[0] // 2
    for slot, kv_ref in zip(slots, kv_refs):
        for side in range(2):
            pay_ref = pay_refs[side]

            @pl.when(listed_pair(pay_ref, rows, side, slot))
            def _():
                write_bias(bias_ref, start_ref, side, slot)

                def body(head, carry):
                    row = pl.ds(side * heads + head, 1)
                    scores = nt_dot(kv_ref[:, 0:HD], pay_ref[0:rows, head_cols(head)])
                    scores = scores * SCORE_SCALE + bias_ref[...]
                    old_max = m_ref[row, :]
                    new_max = jnp.maximum(old_max, jnp.max(scores, axis=0, keepdims=True))
                    total = jnp.sum(jnp.exp2(scores - new_max), axis=0, keepdims=True)
                    l_ref[row, :] = l_ref[row, :] * jnp.exp2(old_max - new_max) + total
                    m_ref[row, :] = new_max
                    return carry

                lax.fori_loop(0, heads, body, 0, unroll=2)


def stats_near_kernel(doc_ref, own_ref, par_ref, kv0_ref, kv1_ref, kv2_ref, start_ref, m_ref, l_ref, bias_ref):
    rows = bias_ref.shape[0]
    lanes = lax.broadcasted_iota(jnp.int32, (1, rows), 1)
    positions = [side_block(side) * rows + lanes for side in range(2)]

    def step(doc, carry):
        end, first, second = carry
        end = end + doc_ref[doc]
        return (end, jnp.where(end <= positions[0], end, first), jnp.where(end <= positions[1], end, second))

    zero = jnp.zeros((1, rows), jnp.int32)
    _, first, second = lax.fori_loop(0, doc_ref.shape[0], step, (jnp.int32(0), zero, zero))
    start_ref[...] = jnp.zeros_like(start_ref)
    start_ref[0:1, :] = first
    start_ref[1:2, :] = second
    m_ref[...] = jnp.full_like(m_ref, EMPTY)
    l_ref[...] = jnp.zeros_like(l_ref)
    stats_slots((0, 1, 2), (kv0_ref, kv1_ref, kv2_ref), (own_ref, par_ref), start_ref, m_ref, l_ref, bias_ref)


def stats_far_kernel(own_ref, par_ref, start_ref, m_in, l_in, delta_ref, kv3_ref, kv4_ref, out_ref, m_ref, l_ref, bias_ref):
    m_ref[...] = m_in[...]
    l_ref[...] = l_in[...]
    stats_slots((3, 4), (kv3_ref, kv4_ref), (own_ref, par_ref), start_ref, m_ref, l_ref, bias_ref)
    stat_rows = m_ref.shape[0]
    total = l_ref[...]
    some = total > 0.0
    out_ref[0:stat_rows, :] = jnp.where(some, m_ref[...] + jnp.log2(jnp.where(some, total, 1.0)), EMPTY)
    out_ref[stat_rows:, :] = delta_ref[...]


def combine_stats(mine_ref, other_ref, lse_ref, delta_ref):
    heads = delta_ref.shape[0] // 2
    for side in range(2):
        a = mine_ref[side * heads : (side + 1) * heads, :]
        b = other_ref[(1 - side) * heads : (2 - side) * heads, :]
        top = jnp.maximum(a, b)
        lse_ref[side * heads : (side + 1) * heads, :] = top + jnp.log2(jnp.exp2(a - top) + jnp.exp2(b - top))
    delta_ref[0:heads, :] = mine_ref[2 * heads :, :]
    delta_ref[heads:, :] = other_ref[2 * heads :, :]


def grad_slot(slot, kv_ref, pay_refs, start_ref, lse_ref, delta_ref, dq_ref, bias_ref, kt_ref, dk_ref, dv_ref):
    rows = bias_ref.shape[0]
    heads = lse_ref.shape[0] // 2
    dk_ref[...] = jnp.zeros_like(dk_ref)
    dv_ref[...] = jnp.zeros_like(dv_ref)
    kt_ref[...] = kv_ref[:, 0:HD].T
    for side in range(2):
        pay_ref = pay_refs[side]
        width = pay_ref.shape[1] // 2

        @pl.when(listed_pair(pay_ref, rows, side, slot))
        def _():
            write_bias(bias_ref, start_ref, side, slot)

            def body(head, carry):
                row = pl.ds(side * heads + head, 1)
                q_head = pay_ref[0:rows, head_cols(head)]
                g_head = pay_ref[0:rows, head_cols(head + width // HD)]
                scores = nt_dot(kv_ref[:, 0:HD], q_head) * SCORE_SCALE + bias_ref[...]
                probs = jnp.exp2(scores - lse_ref[row, :])
                d_prob = nt_dot(kv_ref[:, HD:], g_head)
                d_score = (probs * (d_prob - delta_ref[row, :])).astype(jnp.bfloat16)
                dv_ref[...] += nn_dot(probs.astype(jnp.bfloat16), g_head)
                dk_ref[...] += nn_dot(d_score, q_head)
                at = pl.ds(pl.multiple_of((side * heads + head) * HD, HD), HD)
                dq_ref[at, :] += nn_dot(kt_ref[...], d_score)
                return carry

            lax.fori_loop(0, heads, body, 0, unroll=2)


def write_piece(out_ref, dk_ref, dv_ref):
    out_ref[:, 0:HD] = (dk_ref[...] * FACTOR).astype(out_ref.dtype)
    out_ref[:, HD:] = dv_ref[...].astype(out_ref.dtype)


def grad_far_kernel(own_ref, par_ref, start_ref, mine_ref, other_ref, kv3_ref, kv4_ref, p3_ref, p4_ref, dq_ref,
                    lse_ref, delta_ref, bias_ref, kt_ref, dk_ref, dv_ref):
    combine_stats(mine_ref, other_ref, lse_ref, delta_ref)
    dq_ref[...] = jnp.zeros_like(dq_ref)
    for slot, kv_ref, out_ref in ((4, kv4_ref, p4_ref), (3, kv3_ref, p3_ref)):
        grad_slot(slot, kv_ref, (own_ref, par_ref), start_ref, lse_ref, delta_ref, dq_ref, bias_ref, kt_ref, dk_ref, dv_ref)
        write_piece(out_ref, dk_ref, dv_ref)


def grad_near_kernel(own_ref, par_ref, start_ref, mine_ref, other_ref, kv0_ref, kv1_ref, kv2_ref, dq_in,
                     p0_ref, p1_ref, p2_ref, dq_own_ref, dq_par_ref,
                     lse_ref, delta_ref, bias_ref, kt_ref, dk_ref, dv_ref, dq_ref):
    combine_stats(mine_ref, other_ref, lse_ref, delta_ref)
    dq_ref[...] = dq_in[...]
    for slot, kv_ref, out_ref in ((2, kv2_ref, p2_ref), (1, kv1_ref, p1_ref), (0, kv0_ref, p0_ref)):
        grad_slot(slot, kv_ref, (own_ref, par_ref), start_ref, lse_ref, delta_ref, dq_ref, bias_ref, kt_ref, dk_ref, dv_ref)
        write_piece(out_ref, dk_ref, dv_ref)
    heads = lse_ref.shape[0] // 2
    for side, out_ref in ((0, dq_own_ref), (1, dq_par_ref)):
        for head in range(heads):
            at = (side * heads + head) * HD
            block = dq_ref[at : at + HD, :] * FACTOR
            out_ref[:, head * HD : (head + 1) * HD] = block.T.astype(out_ref.dtype)


def call(kernel, in_spaces, outs, scratch, flops, transcendentals, *args):
    moved = sum(a.size * a.dtype.itemsize for a in args) + sum(o.size * o.dtype.itemsize for o in outs)
    return pl.pallas_call(
        kernel,
        out_shape=outs,
        in_specs=[pl.BlockSpec(memory_space=space) for space in in_spaces],
        out_specs=[pl.BlockSpec(memory_space=pltpu.VMEM) for _ in outs],
        scratch_shapes=scratch,
        compiler_params=pltpu.CompilerParams(vmem_limit_bytes=VMEM_BYTES),
        cost_estimate=pl.CostEstimate(flops=flops, bytes_accessed=moved, transcendentals=transcendentals),
    )(*args)


def on_device(queries, keys, values, outputs, out_grad, doc_lengths, block_offsets):
    rows, width = queries.shape
    heads = width // HD
    struct = jax.ShapeDtypeStruct
    f32, bf16 = jnp.float32, jnp.bfloat16
    vmem, smem = pltpu.VMEM, pltpu.SMEM
    pair = 2 * heads * rows * rows

    kv = jnp.concatenate([keys, values], axis=1)
    kv2 = shift(kv, 4)
    kv1 = shift(kv, 2)
    pay, delta = call(
        prep_kernel, [vmem] * 4, [struct((rows + 16, 2 * width), bf16), struct((heads, rows), f32)], [],
        2 * rows * width, 0, queries, out_grad, outputs, block_offsets)
    par = exchange(pay)
    kv3 = shift(kv2, 2)
    kv4 = shift(kv2, 4, 1)

    stat = struct((2 * heads, rows), f32)
    bias = pltpu.VMEM((rows, rows), f32)
    start, m_near, l_near = call(
        stats_near_kernel, [smem] + [vmem] * 5, [struct((8, rows), jnp.int32), stat, stat], [bias],
        3 * pair * HD * 2, 3 * pair, doc_lengths, pay, par, kv, kv1, kv2)
    stat_scratch = pltpu.VMEM((2 * heads, rows), f32)
    (mine,) = call(
        stats_far_kernel, [vmem] * 8, [struct((3 * heads, rows), f32)], [stat_scratch, stat_scratch, bias],
        2 * pair * HD * 2, 2 * pair, pay, par, start, m_near, l_near, delta, kv3, kv4)
    other = exchange(mine)

    part = pltpu.VMEM((rows, HD), f32)
    scratch = [stat_scratch, stat_scratch, bias, pltpu.VMEM((HD, rows), bf16), part, part]
    piece16, piece32 = struct((rows, 2 * HD), bf16), struct((rows, 2 * HD), f32)
    dq_shape = (2 * width, rows)
    p3, p4, dq = call(
        grad_far_kernel, [vmem] * 7, [piece16, piece16, struct(dq_shape, f32)], scratch,
        2 * 5 * pair * HD * 2, 2 * pair, pay, par, start, mine, other, kv3, kv4)
    back4 = shift(p4, -4, 1)
    back3 = shift(p3, -2)
    p0, p1, p2, dq_own, dq_par = call(
        grad_near_kernel, [vmem] * 9,
        [piece32, piece16, piece32, struct((rows, width), f32), struct((rows, width), bf16)],
        scratch + [pltpu.VMEM(dq_shape, f32)],
        3 * 5 * pair * HD * 2, 3 * pair, pay, par, start, mine, other, kv, kv1, kv2, dq)
    back1 = shift(p1, -2)
    dq_other = exchange(dq_par)
    p2_sum = (p2 + back3.astype(f32) + back4.astype(f32)).astype(bf16)
    back2 = shift(p2_sum, -4)
    grad_queries = (dq_own + dq_other.astype(f32)).astype(bf16)
    summed = p0 + back1.astype(f32) + back2.astype(f32)
    return grad_queries, summed[:, :HD].astype(bf16), summed[:, HD:].astype(bf16)


def solution(mesh):
    tokens = P(("dp", "cp"), "hd")
    return jax.shard_map(
        on_device,
        mesh=mesh,
        in_specs=(tokens, tokens, tokens, tokens, tokens, P("dp"), P(("dp", "cp"), None)),
        out_specs=(tokens, tokens, tokens),
        check_vma=False,
    )
```

```python
import jax
import jax.numpy as jnp
from jax import lax
from jax.experimental import pallas as pl
from jax.experimental.pallas import tpu as pltpu
from jax.sharding import PartitionSpec as P

HD = 128
FACTOR = HD ** (-0.5)
SCORE_SCALE = FACTOR * 1.4426950408889634
MASKED = -1e30
EMPTY = -1e20
VMEM_BYTES = 32 * 1024 * 1024


def shift(array, by, parity=None):
    n = lax.axis_size("cp")
    pairs = [(i, (i + by) % n) for i in range(n) if parity is None or i % 2 == parity]
    return lax.ppermute(array, "cp", pairs)


def exchange(array):
    n = lax.axis_size("cp")
    return lax.ppermute(array, "cp", [(i, i ^ 1) for i in range(n)])


def nt_dot(a, b):
    return lax.dot_general(a, b, (((1,), (1,)), ((), ())), preferred_element_type=jnp.float32)


def nn_dot(a, b):
    return lax.dot_general(a, b, (((1,), (0,)), ((), ())), preferred_element_type=jnp.float32)


def side_block(side):
    block = lax.axis_index("cp")
    if side == 0:
        return block
    return block + 1 - 2 * lax.rem(block, 2)


def side_refs(ref):
    core = lax.rem(lax.axis_index("cp"), 2)
    return ref.at[core], ref.at[1 - core]


def listed_pair(off_ref, side, slot):
    key_block = lax.axis_index("cp") - 2 * slot
    block = side_block(side)
    hits = jnp.max((off_ref[lax.rem(block, 2)] == block - key_block).astype(jnp.float32))
    return (hits > 0.0) & (block >= key_block) & (key_block >= 0)


def write_bias(bias_ref, start_ref, side, slot):
    rows = bias_ref.shape[0]
    key_pos = (lax.axis_index("cp") - 2 * slot) * rows + lax.broadcasted_iota(jnp.int32, bias_ref.shape, 0)
    q_pos = side_block(side) * rows + lax.broadcasted_iota(jnp.int32, bias_ref.shape, 1)
    allowed = (key_pos >= start_ref[side : side + 1, :]) & (key_pos <= q_pos)
    bias_ref[...] = jnp.where(allowed, 0.0, MASKED)


def prep_kernel(doc_ref, gs_ref, o_ref, start_ref, delta_ref):
    g_ref = side_refs(gs_ref)[0]
    rows, width = o_ref.shape
    lanes = lax.broadcasted_iota(jnp.int32, (1, rows), 1)
    positions = [side_block(side) * rows + lanes for side in range(2)]

    def step(doc, carry):
        end, first, second = carry
        end = end + doc_ref[doc]
        return (end, jnp.where(end <= positions[0], end, first), jnp.where(end <= positions[1], end, second))

    zero = jnp.zeros((1, rows), jnp.int32)
    _, first, second = lax.fori_loop(0, doc_ref.shape[0], step, (jnp.int32(0), zero, zero))
    start_ref[...] = jnp.zeros_like(start_ref)
    start_ref[0:1, :] = first
    start_ref[1:2, :] = second
    for head in range(width // HD):
        cols = slice(head * HD, (head + 1) * HD)
        product = g_ref[:, cols].astype(jnp.float32) * o_ref[:, cols].astype(jnp.float32)
        delta_ref[head : head + 1, :] = jnp.sum(product.T, axis=0, keepdims=True)


def stats_slots(first, kv_ref, q_refs, off_ref, start_ref, m_ref, l_ref, bias_ref):
    rows = bias_ref.shape[0]
    heads = m_ref.shape[0] // 2
    for side, q_ref in enumerate(q_refs):

        def step(i, carry, side=side, q_ref=q_ref):
            @pl.when(listed_pair(off_ref, side, first + i))
            def _():
                write_bias(bias_ref, start_ref, side, first + i)
                keys = kv_ref[i, 0]

                def products(head):
                    return nt_dot(keys, q_ref[:, head * HD : (head + 1) * HD])

                ahead = products(0)
                for head in range(heads):
                    scores = ahead * SCORE_SCALE + bias_ref[...]
                    if head + 1 < heads:
                        ahead = products(head + 1)
                    row = slice(side * heads + head, side * heads + head + 1)
                    old_max = m_ref[row, :]
                    new_max = jnp.maximum(old_max, jnp.max(scores, axis=0, keepdims=True))
                    total = jnp.sum(jnp.exp2(scores - new_max), axis=0, keepdims=True)
                    l_ref[row, :] = l_ref[row, :] * jnp.exp2(old_max - new_max) + total
                    m_ref[row, :] = new_max

            return carry

        lax.fori_loop(0, kv_ref.shape[0], step, 0)


def stats_near_kernel(qs_ref, off_ref, start_ref, kv0_ref, kv1_ref, kv2_ref, m_ref, l_ref, bias_ref, kv_ref):
    m_ref[...] = jnp.full_like(m_ref, EMPTY)
    l_ref[...] = jnp.zeros_like(l_ref)
    for i, ref in enumerate((kv0_ref, kv1_ref, kv2_ref)):
        kv_ref[i] = ref[...]
    stats_slots(0, kv_ref, side_refs(qs_ref), off_ref, start_ref, m_ref, l_ref, bias_ref)


def stats_far_kernel(qs_ref, off_ref, start_ref, m_in, l_in, delta_ref, kv3_ref, kv4_ref, out_ref,
                     m_ref, l_ref, bias_ref, kv_ref):
    m_ref[...] = m_in[...]
    l_ref[...] = l_in[...]
    kv_ref[0] = kv3_ref[...]
    kv_ref[1] = kv4_ref[...]
    stats_slots(3, kv_ref, side_refs(qs_ref), off_ref, start_ref, m_ref, l_ref, bias_ref)
    stat_rows = m_ref.shape[0]
    total = l_ref[...]
    some = total > 0.0
    out_ref[0:stat_rows, :] = jnp.where(some, m_ref[...] + jnp.log2(jnp.where(some, total, 1.0)), EMPTY)
    out_ref[stat_rows:, :] = delta_ref[...]


def combine_stats(stats_ref, lse_ref, delta_ref):
    heads = delta_ref.shape[0] // 2
    core = lax.rem(lax.axis_index("cp"), 2)
    mine, other = stats_ref[core], stats_ref[1 - core]
    for side in range(2):
        a = mine[side * heads : (side + 1) * heads]
        b = other[(1 - side) * heads : (2 - side) * heads]
        top = jnp.maximum(a, b)
        lse_ref[side * heads : (side + 1) * heads, :] = top + jnp.log2(jnp.exp2(a - top) + jnp.exp2(b - top))
    delta_ref[0:heads, :] = mine[2 * heads :]
    delta_ref[heads:, :] = other[2 * heads :]


def grad_slots(first, kv_ref, q_refs, g_refs, off_ref, start_ref, lse_ref, delta_ref, dq_ref, bias_ref, part_ref):
    rows = bias_ref.shape[0]
    heads = lse_ref.shape[0] // 2
    part_ref[...] = jnp.zeros_like(part_ref)
    for side, (q_ref, g_ref) in enumerate(zip(q_refs, g_refs)):

        def step(i, carry, side=side, q_ref=q_ref, g_ref=g_ref):
            @pl.when(listed_pair(off_ref, side, first + i))
            def _():
                write_bias(bias_ref, start_ref, side, first + i)
                keys = kv_ref[i, 0]
                values = kv_ref[i, 1]
                keys_t = keys.T

                def q_head(head):
                    return q_ref[:, head * HD : (head + 1) * HD]

                def g_head(head):
                    return g_ref[:, head * HD : (head + 1) * HD]

                def products(head):
                    return nt_dot(keys, q_head(head)), nt_dot(values, g_head(head))

                def weights(head, ahead):
                    row = slice(side * heads + head, side * heads + head + 1)
                    probs = jnp.exp2(ahead[0] * SCORE_SCALE + bias_ref[...] - lse_ref[row, :])
                    d_score = probs * (ahead[1] - delta_ref[row, :])
                    return probs.astype(jnp.bfloat16), d_score.astype(jnp.bfloat16)

                def sums(head, pair, acc):
                    at = (side * heads + head) * HD
                    dq_ref[at : at + HD, :] += nn_dot(keys_t, pair[1])
                    return acc[0] + nn_dot(pair[1], q_head(head)), acc[1] + nn_dot(pair[0], g_head(head))

                acc = (part_ref[i, :, 0:HD], part_ref[i, :, HD:])
                ahead, pair = products(0), None
                for head in range(heads):
                    following = products(head + 1) if head + 1 < heads else None
                    if pair is not None:
                        acc = sums(head - 1, pair, acc)
                    pair, ahead = weights(head, ahead), following
                acc = sums(heads - 1, pair, acc)
                part_ref[i, :, 0:HD] = acc[0]
                part_ref[i, :, HD:] = acc[1]

            return carry

        lax.fori_loop(0, kv_ref.shape[0], step, 0)


def write_piece(out_ref, part):
    out_ref[:, 0:HD] = (part[:, 0:HD] * FACTOR).astype(out_ref.dtype)
    out_ref[:, HD:] = part[:, HD:].astype(out_ref.dtype)


def grad_far_kernel(qs_ref, gs_ref, off_ref, start_ref, stats_ref, kv3_ref, kv4_ref, p3_ref, p4_ref, dq_ref,
                    lse_ref, delta_ref, bias_ref, kv_ref, part_ref):
    combine_stats(stats_ref, lse_ref, delta_ref)
    dq_ref[...] = jnp.zeros_like(dq_ref)
    kv_ref[0] = kv3_ref[...]
    kv_ref[1] = kv4_ref[...]
    grad_slots(3, kv_ref, side_refs(qs_ref), side_refs(gs_ref), off_ref, start_ref, lse_ref, delta_ref, dq_ref, bias_ref, part_ref)
    write_piece(p3_ref, part_ref[0])
    write_piece(p4_ref, part_ref[1])


def grad_mid_kernel(qs_ref, gs_ref, off_ref, start_ref, stats_ref, kv1_ref, kv2_ref, dq_in, p1_ref, p2_ref, dq_ref,
                    lse_ref, delta_ref, bias_ref, kv_ref, part_ref):
    combine_stats(stats_ref, lse_ref, delta_ref)
    dq_ref[...] = dq_in[...]
    kv_ref[0] = kv1_ref[...]
    kv_ref[1] = kv2_ref[...]
    grad_slots(1, kv_ref, side_refs(qs_ref), side_refs(gs_ref), off_ref, start_ref, lse_ref, delta_ref, dq_ref, bias_ref, part_ref)
    write_piece(p1_ref, part_ref[0])
    write_piece(p2_ref, part_ref[1])


def grad_own_kernel(qs_ref, gs_ref, off_ref, start_ref, stats_ref, kv0_ref, dq_in, p0_ref, dq_own_ref, dq_par_ref,
                    lse_ref, delta_ref, bias_ref, kv_ref, part_ref, dq_ref):
    combine_stats(stats_ref, lse_ref, delta_ref)
    dq_ref[...] = dq_in[...]
    kv_ref[0] = kv0_ref[...]
    grad_slots(0, kv_ref, side_refs(qs_ref), side_refs(gs_ref), off_ref, start_ref, lse_ref, delta_ref, dq_ref, bias_ref, part_ref)
    write_piece(p0_ref, part_ref[0])
    heads = lse_ref.shape[0] // 2
    for side, out_ref in ((0, dq_own_ref), (1, dq_par_ref)):
        for head in range(heads):
            at = (side * heads + head) * HD
            block = dq_ref[at : at + HD, :] * FACTOR
            out_ref[:, head * HD : (head + 1) * HD] = block.T.astype(out_ref.dtype)


def call(kernel, in_spaces, outs, scratch, flops, transcendentals, *args):
    moved = sum(a.size * a.dtype.itemsize for a in args) + sum(o.size * o.dtype.itemsize for o in outs)
    return pl.pallas_call(
        kernel,
        out_shape=outs,
        in_specs=[pl.BlockSpec(memory_space=space) for space in in_spaces],
        out_specs=[pl.BlockSpec(memory_space=pltpu.VMEM) for _ in outs],
        scratch_shapes=scratch,
        compiler_params=pltpu.CompilerParams(vmem_limit_bytes=VMEM_BYTES),
        cost_estimate=pl.CostEstimate(flops=flops, bytes_accessed=moved, transcendentals=transcendentals),
    )(*args)


def on_device(queries, keys, values, outputs, out_grad, doc_lengths, block_offsets):
    rows, width = queries.shape
    heads = width // HD
    struct = jax.ShapeDtypeStruct
    f32, bf16 = jnp.float32, jnp.bfloat16
    vmem, smem = pltpu.VMEM, pltpu.SMEM
    pair = 2 * heads * rows * rows

    pairs = [[i, i + 1] for i in range(0, lax.axis_size("cp"), 2)]
    which = lax.broadcasted_iota(jnp.int32, (2, rows, HD), 0)
    kv = jnp.where(which == 0, keys[None], values[None])
    kv2 = shift(kv, 4)
    kv1 = shift(kv, 2)
    offsets = lax.all_gather(block_offsets, "cp", axis_index_groups=pairs)
    qs = lax.all_gather(queries, "cp", axis_index_groups=pairs)
    gs = lax.all_gather(out_grad, "cp", axis_index_groups=pairs)
    kv2, kv1, qs, gs, offsets = lax.optimization_barrier((kv2, kv1, qs, gs, offsets))
    stat = struct((2 * heads, rows), f32)
    stat_scratch = pltpu.VMEM((2 * heads, rows), f32)
    bias = pltpu.VMEM((rows, rows), f32)

    def stack(count):
        return pltpu.VMEM((count, 2, rows, HD), bf16)

    def parts(count):
        return pltpu.VMEM((count, rows, 2 * HD), f32)

    start, delta = call(
        prep_kernel, [smem] + [vmem] * 2, [struct((8, rows), jnp.int32), struct((heads, rows), f32)], [],
        2 * rows * width, 0, doc_lengths, gs, outputs)
    kv3 = shift(kv2, 2)
    kv4 = shift(kv2, 4, 1)
    q_side = (qs, offsets, start)
    m_near, l_near = call(
        stats_near_kernel, [vmem] * 6, [stat, stat], [bias, stack(3)],
        3 * pair * HD * 2, 3 * pair, *q_side, kv, kv1, kv2)
    (mine,) = call(
        stats_far_kernel, [vmem] * 8, [struct((3 * heads, rows), f32)], [stat_scratch, stat_scratch, bias, stack(2)],
        2 * pair * HD * 2, 2 * pair, *q_side, m_near, l_near, delta, kv3, kv4)
    stats = lax.all_gather(mine, "cp", axis_index_groups=pairs)

    scratch = [stat_scratch, stat_scratch, bias]
    piece16, piece32 = struct((rows, 2 * HD), bf16), struct((rows, 2 * HD), f32)
    dq_shape = (2 * width, rows)
    sides = (qs, gs, offsets, start, stats)
    p3, p4, dq = call(
        grad_far_kernel, [vmem] * 7, [piece16, piece16, struct(dq_shape, f32)], scratch + [stack(2), parts(2)],
        2 * 5 * pair * HD * 2, 2 * pair, *sides, kv3, kv4)
    back4 = shift(p4, -4, 1)
    back3 = shift(p3, -2)
    p1, p2, dq = call(
        grad_mid_kernel, [vmem] * 8, [piece16, piece32, struct(dq_shape, f32)], scratch + [stack(2), parts(2)],
        2 * 5 * pair * HD * 2, 2 * pair, *sides, kv1, kv2, dq)
    p2_sum = (p2 + back3.astype(f32) + back4.astype(f32)).astype(bf16)
    back2 = shift(p2_sum, -4)
    back1 = shift(p1, -2)
    p0, dq_own, dq_par = call(
        grad_own_kernel, [vmem] * 7, [piece32, struct((rows, width), f32), struct((rows, width), bf16)],
        scratch + [stack(1), parts(1), pltpu.VMEM(dq_shape, f32)],
        5 * pair * HD * 2, pair, *sides, kv, dq)
    dq_other = exchange(dq_par)
    grad_queries = (dq_own + dq_other.astype(f32)).astype(bf16)
    summed = p0 + back1.astype(f32) + back2.astype(f32)
    return grad_queries, summed[:, :HD].astype(bf16), summed[:, HD:].astype(bf16)


def solution(mesh):
    tokens = P(("dp", "cp"), "hd")
    return jax.shard_map(
        on_device,
        mesh=mesh,
        in_specs=(tokens, tokens, tokens, tokens, tokens, P("dp"), P(("dp", "cp"), None)),
        out_specs=(tokens, tokens, tokens),
        check_vma=False,
    )
```

```python
import jax
import jax.numpy as jnp
from jax import lax
from jax.experimental import pallas as pl
from jax.experimental.pallas import tpu as pltpu
from jax.sharding import PartitionSpec as P

HD = 128
FACTOR = HD ** (-0.5)
SCORE_SCALE = FACTOR * 1.4426950408889634
MASKED = -1e30
EMPTY = -1e20
VMEM_BYTES = 32 * 1024 * 1024


def shift(array, by, parity=None):
    n = lax.axis_size("cp")
    pairs = [(i, (i + by) % n) for i in range(n) if parity is None or i % 2 == parity]
    return lax.ppermute(array, "cp", pairs)


def gather_pair(array):
    n = lax.axis_size("cp")
    return lax.all_gather(array, "cp", axis_index_groups=[[i, i + 1] for i in range(0, n, 2)])


def nt_dot(a, b):
    return lax.dot_general(a, b, (((1,), (1,)), ((), ())), preferred_element_type=jnp.float32)


def nn_dot(a, b):
    return lax.dot_general(a, b, (((1,), (0,)), ((), ())), preferred_element_type=jnp.float32)


def core_parity():
    return lax.rem(lax.axis_index("cp"), 2)


def key_block(slot, entry):
    return lax.axis_index("cp") - core_parity() + 1 - 2 * slot - entry


def listed(off_ref, slot, entry):
    block = lax.axis_index("cp")
    key = key_block(slot, entry)
    hits = jnp.max((off_ref[...] == block - key).astype(jnp.float32))
    return (hits > 0.0) & (block >= key) & (key >= 0)


def write_bias(bias_ref, start_ref, slot, entry):
    rows = bias_ref.shape[0]
    key_pos = key_block(slot, entry) * rows + lax.broadcasted_iota(jnp.int32, bias_ref.shape, 0)
    q_pos = lax.axis_index("cp") * rows + lax.broadcasted_iota(jnp.int32, bias_ref.shape, 1)
    allowed = (key_pos >= start_ref[0:1, :]) & (key_pos <= q_pos)
    bias_ref[...] = jnp.where(allowed, 0.0, MASKED)


def prep_kernel(doc_ref, g_ref, o_ref, start_ref, delta_ref):
    rows, width = g_ref.shape
    positions = lax.axis_index("cp") * rows + lax.broadcasted_iota(jnp.int32, (8, rows), 1)

    def step(doc, carry):
        end, first = carry
        end = end + doc_ref[doc]
        return (end, jnp.where(end <= positions, end, first))

    _, first = lax.fori_loop(0, doc_ref.shape[0], step, (jnp.int32(0), jnp.zeros((8, rows), jnp.int32)))
    start_ref[...] = first
    for head in range(width // HD):
        cols = slice(head * HD, (head + 1) * HD)
        product = g_ref[:, cols].astype(jnp.float32) * o_ref[:, cols].astype(jnp.float32)
        delta_ref[head : head + 1, :] = jnp.sum(product.T, axis=0, keepdims=True)


def load_entries(kv_ref, gathered):
    for i in range(kv_ref.shape[0]):
        pair = gathered[i // 2]
        kv_ref[i] = pair[1 - i % 2] if len(pair.shape) == 4 else pair[...]


def stats_entries(slot, kv_ref, q_ref, off_ref, start_ref, m_ref, l_ref, bias_ref):
    heads = m_ref.shape[0]

    def step(entry, carry):
        @pl.when(listed(off_ref, slot, entry))
        def _():
            write_bias(bias_ref, start_ref, slot, entry)
            keys = kv_ref[entry, 0]

            def products(head):
                return nt_dot(keys, q_ref[:, head * HD : (head + 1) * HD])

            ahead = products(0)
            for head in range(heads):
                scores = ahead * SCORE_SCALE + bias_ref[...]
                if head + 1 < heads:
                    ahead = products(head + 1)
                row = slice(head, head + 1)
                old_max = m_ref[row, :]
                new_max = jnp.maximum(old_max, jnp.max(scores, axis=0, keepdims=True))
                total = jnp.sum(jnp.exp2(scores - new_max), axis=0, keepdims=True)
                l_ref[row, :] = l_ref[row, :] * jnp.exp2(old_max - new_max) + total
                m_ref[row, :] = new_max

        return carry

    lax.fori_loop(0, kv_ref.shape[0], step, 0)


def stats_own_kernel(q_ref, off_ref, start_ref, kv0, m_ref, l_ref, bias_ref, kv_ref):
    m_ref[...] = jnp.full_like(m_ref, EMPTY)
    l_ref[...] = jnp.zeros_like(l_ref)
    load_entries(kv_ref, (kv0,))
    stats_entries(0, kv_ref, q_ref, off_ref, start_ref, m_ref, l_ref, bias_ref)


def stats_mid_kernel(q_ref, off_ref, start_ref, m_in, l_in, kv1, kv2, m_ref, l_ref, bias_ref, kv_ref):
    m_ref[...] = m_in[...]
    l_ref[...] = l_in[...]
    load_entries(kv_ref, (kv1, kv2))
    stats_entries(1, kv_ref, q_ref, off_ref, start_ref, m_ref, l_ref, bias_ref)


def grad_entries(slot, kv_ref, q_ref, g_ref, off_ref, start_ref, lse_ref, delta_ref, dq_ref, bias_ref, part_ref):
    heads = lse_ref.shape[0]
    part_ref[...] = jnp.zeros_like(part_ref)

    def step(entry, carry):
        @pl.when(listed(off_ref, slot, entry))
        def _():
            write_bias(bias_ref, start_ref, slot, entry)
            keys = kv_ref[entry, 0]
            values = kv_ref[entry, 1]
            keys_t = keys.T

            def q_head(head):
                return q_ref[:, head * HD : (head + 1) * HD]

            def g_head(head):
                return g_ref[:, head * HD : (head + 1) * HD]

            def products(head):
                return nt_dot(keys, q_head(head)), nt_dot(values, g_head(head))

            def weights(head, ahead):
                row = slice(head, head + 1)
                probs = jnp.exp2(ahead[0] * SCORE_SCALE + bias_ref[...] - lse_ref[row, :])
                d_score = probs * (ahead[1] - delta_ref[row, :])
                return probs.astype(jnp.bfloat16), d_score.astype(jnp.bfloat16)

            def sums(head, pair, acc):
                at = head * HD
                dq_ref[at : at + HD, :] += nn_dot(keys_t, pair[1])
                d_key = nn_dot(pair[1], q_head(head))
                d_value = nn_dot(pair[0], g_head(head))
                return (d_key, d_value) if acc is None else (acc[0] + d_key, acc[1] + d_value)

            acc = None
            ahead, pair = products(0), None
            for head in range(heads):
                following = products(head + 1) if head + 1 < heads else None
                if pair is not None:
                    acc = sums(head - 1, pair, acc)
                pair, ahead = weights(head, ahead), following
            acc = sums(heads - 1, pair, acc)
            part_ref[entry, :, 0:HD] = acc[0] * FACTOR
            part_ref[entry, :, HD:] = acc[1]

        return carry

    lax.fori_loop(0, kv_ref.shape[0], step, 0)


def grad_far_kernel(q_ref, g_ref, off_ref, start_ref, delta_ref, m_in, l_in, kv3, kv4,
                    p3_own, p3_other, p4_ref, dq_ref, lse_ref, m_ref, l_ref, bias_ref, kv_ref, part_ref):
    m_ref[...] = m_in[...]
    l_ref[...] = l_in[...]
    load_entries(kv_ref, (kv3, kv4))
    stats_entries(3, kv_ref, q_ref, off_ref, start_ref, m_ref, l_ref, bias_ref)
    lse_ref[...] = m_ref[...] + jnp.log2(l_ref[...])
    dq_ref[...] = jnp.zeros_like(dq_ref)
    grad_entries(3, kv_ref, q_ref, g_ref, off_ref, start_ref, lse_ref, delta_ref, dq_ref, bias_ref, part_ref)
    core = core_parity()
    p3_own[...] = part_ref[1 - core]
    p3_other[...] = part_ref[core].astype(p3_other.dtype)
    p4_ref[...] = part_ref[2].astype(p4_ref.dtype)


def grad_mid_kernel(q_ref, g_ref, off_ref, start_ref, delta_ref, lse_ref, kv1, kv2, dq_in,
                    p_own, p_other, dq_ref, bias_ref, kv_ref, part_ref):
    load_entries(kv_ref, (kv1, kv2))
    dq_ref[...] = dq_in[...]
    grad_entries(1, kv_ref, q_ref, g_ref, off_ref, start_ref, lse_ref, delta_ref, dq_ref, bias_ref, part_ref)
    core = core_parity()
    for i in range(2):
        p_own[i] = part_ref[2 * i + 1 - core]
        p_other[i] = part_ref[2 * i + core].astype(p_other.dtype)


def grad_own_kernel(q_ref, g_ref, off_ref, start_ref, delta_ref, lse_ref, kv0, dq_in,
                    p_own, p_other, out_ref, bias_ref, kv_ref, part_ref, dq_ref):
    load_entries(kv_ref, (kv0,))
    dq_ref[...] = dq_in[...]
    grad_entries(0, kv_ref, q_ref, g_ref, off_ref, start_ref, lse_ref, delta_ref, dq_ref, bias_ref, part_ref)
    core = core_parity()
    p_own[...] = part_ref[1 - core]
    p_other[...] = part_ref[core].astype(p_other.dtype)
    for head in range(lse_ref.shape[0]):
        at = slice(head * HD, (head + 1) * HD)
        out_ref[:, at] = (dq_ref[at, :] * FACTOR).T.astype(out_ref.dtype)


def merge_far_kernel(own_ref, gathered_ref, out_ref):
    total = own_ref[...] + gathered_ref[1 - core_parity()].astype(jnp.float32)
    out_ref[...] = total.astype(out_ref.dtype)


def merge_mid_kernel(own_ref, gathered_ref, back3_ref, back4_ref, p1_ref, p2_ref):
    other = gathered_ref.at[1 - core_parity()]
    p1_ref[...] = (own_ref[0] + other[0].astype(jnp.float32)).astype(p1_ref.dtype)
    total = own_ref[1] + other[1].astype(jnp.float32)
    total += back3_ref[...].astype(jnp.float32) + back4_ref[...].astype(jnp.float32)
    p2_ref[...] = total.astype(p2_ref.dtype)


def final_kernel(own_ref, gathered_ref, back1_ref, back2_ref, dk_ref, dv_ref):
    total = own_ref[...] + gathered_ref[1 - core_parity()].astype(jnp.float32)
    total += back1_ref[...].astype(jnp.float32) + back2_ref[...].astype(jnp.float32)
    dk_ref[...] = total[:, 0:HD].astype(dk_ref.dtype)
    dv_ref[...] = total[:, HD:].astype(dv_ref.dtype)


def call(kernel, outs, scratch, units, *args, smem_args=0):
    pair = 2 * 8 * 256 * 256
    moved = sum(a.size * a.dtype.itemsize for a in args) + sum(o.size * o.dtype.itemsize for o in outs)
    spaces = [pltpu.SMEM] * smem_args + [pltpu.VMEM] * (len(args) - smem_args)
    return pl.pallas_call(
        kernel,
        out_shape=outs,
        in_specs=[pl.BlockSpec(memory_space=space) for space in spaces],
        out_specs=[pl.BlockSpec(memory_space=pltpu.VMEM) for _ in outs],
        scratch_shapes=scratch,
        compiler_params=pltpu.CompilerParams(vmem_limit_bytes=VMEM_BYTES),
        cost_estimate=pl.CostEstimate(flops=units * pair * HD, bytes_accessed=moved, transcendentals=pair),
    )(*args)


def on_device(queries, keys, values, outputs, out_grad, doc_lengths, block_offsets):
    rows, width = queries.shape
    heads = width // HD
    struct = jax.ShapeDtypeStruct
    f32, bf16 = jnp.float32, jnp.bfloat16
    stat = struct((heads, rows), f32)
    piece16, piece32 = struct((rows, 2 * HD), bf16), struct((rows, 2 * HD), f32)
    dq_part = struct((width, rows), f32)
    bias = pltpu.VMEM((rows, rows), f32)
    row_stat = pltpu.VMEM((heads, rows), f32)

    def stack(count):
        return pltpu.VMEM((count, 2, rows, HD), bf16)

    def parts(count):
        return pltpu.VMEM((count, rows, 2 * HD), f32)

    which = lax.broadcasted_iota(jnp.int32, (2, rows, HD), 0)
    kv = jnp.where(which == 0, keys[None], values[None])
    kv2 = shift(kv, 4)
    kv1 = shift(kv, 2)
    both0 = gather_pair(kv)
    start, delta = call(
        prep_kernel, [struct((8, rows), jnp.int32), stat], [], 1, doc_lengths, out_grad, outputs, smem_args=1)
    m, l = call(
        stats_own_kernel, [stat, stat], [bias, stack(2)], 2, queries, block_offsets, start, both0)
    kv1, kv2, m, l, delta = lax.optimization_barrier((kv1, kv2, m, l, delta))
    kv3 = shift(kv2, 2)
    kv4 = shift(kv2, 3, 1)
    both1, both2 = gather_pair(kv1), gather_pair(kv2)
    m, l = call(
        stats_mid_kernel, [stat, stat], [bias, stack(4)], 4, queries, block_offsets, start, m, l, both1, both2)
    both3 = gather_pair(kv3)

    known = (queries, out_grad, block_offsets, start, delta)
    p3_own, p3_other, p4, dq, lse = call(
        grad_far_kernel, [piece32, piece16, piece16, dq_part, stat], [row_stat, row_stat, bias, stack(3), parts(3)],
        18, *known, m, l, both3, kv4)
    back4 = shift(p4, -3, 0)
    (p3,) = call(merge_far_kernel, [piece16], [], 0, p3_own, gather_pair(p3_other))
    back3 = shift(p3, -2)
    p12_own, p12_other, dq = call(
        grad_mid_kernel, [struct((2, rows, 2 * HD), f32), struct((2, rows, 2 * HD), bf16), dq_part],
        [bias, stack(4), parts(4)], 20, *known, lse, both1, both2, dq)
    p1, p2 = call(merge_mid_kernel, [piece16, piece16], [], 0, p12_own, gather_pair(p12_other), back3, back4)
    back2 = shift(p2, -4)
    back1 = shift(p1, -2)
    p0_own, p0_other, grad_queries = call(
        grad_own_kernel, [piece32, piece16, struct((rows, width), bf16)],
        [bias, stack(2), parts(2), pltpu.VMEM((width, rows), f32)], 10, *known, lse, both0, dq)
    piece = struct((rows, HD), bf16)
    grad_keys, grad_values = call(
        final_kernel, [piece, piece], [], 0, p0_own, gather_pair(p0_other), back1, back2)
    return grad_queries, grad_keys, grad_values


def solution(mesh):
    tokens = P(("dp", "cp"), "hd")
    return jax.shard_map(
        on_device,
        mesh=mesh,
        in_specs=(tokens, tokens, tokens, tokens, tokens, P("dp"), P(("dp", "cp"), None)),
        out_specs=(tokens, tokens, tokens),
        check_vma=False,
    )
```

```python
import jax
import jax.numpy as jnp
from jax import lax
from jax.experimental import pallas as pl
from jax.experimental.pallas import tpu as pltpu
from jax.sharding import PartitionSpec as P

HD = 128
FACTOR = HD ** (-0.5)
SCORE_SCALE = FACTOR * 1.4426950408889634
MASKED = -1e30
EMPTY = -1e20
VMEM_BYTES = 32 * 1024 * 1024


def shift(array, by, parity=None):
    n = lax.axis_size("cp")
    pairs = [(i, (i + by) % n) for i in range(n) if parity is None or i % 2 == parity]
    return lax.ppermute(array, "cp", pairs)


def gather_pair(array):
    n = lax.axis_size("cp")
    return lax.all_gather(array, "cp", axis_index_groups=[[i, i + 1] for i in range(0, n, 2)])


def nt_dot(a, b):
    return lax.dot_general(a, b, (((1,), (1,)), ((), ())), preferred_element_type=jnp.float32)


def nn_dot(a, b):
    return lax.dot_general(a, b, (((1,), (0,)), ((), ())), preferred_element_type=jnp.float32)


def core_parity():
    return lax.rem(lax.axis_index("cp"), 2)


def key_block(slot, entry):
    return lax.axis_index("cp") - core_parity() + 1 - 2 * slot - entry


def listed_bits(off_ref):
    offsets = off_ref[...]
    bits = jnp.where(offsets >= 0, lax.shift_left(jnp.ones_like(offsets), jnp.maximum(offsets, 0)), 0)
    return jnp.sum(bits.astype(jnp.float32)).astype(jnp.int32)


def pick(values, i):
    chosen = values[0]
    for j in range(1, len(values)):
        chosen = jnp.where(i == j, values[j], chosen)
    return chosen


def listed(bits, key):
    block = lax.axis_index("cp")
    bit = lax.shift_right_logical(bits, jnp.maximum(block - key, 0)) & 1
    return (bit == 1) & (block >= key) & (key >= 0)


def write_bias(bias_ref, start_ref, key):
    rows = bias_ref.shape[0]
    key_pos = key * rows + lax.broadcasted_iota(jnp.int32, bias_ref.shape, 0)
    q_pos = lax.axis_index("cp") * rows + lax.broadcasted_iota(jnp.int32, bias_ref.shape, 1)
    allowed = (key_pos >= start_ref[0:1, :]) & (key_pos <= q_pos)
    bias_ref[...] = jnp.where(allowed, 0.0, MASKED)


def prep_kernel(doc_ref, g_ref, o_ref, start_ref, delta_ref):
    rows, width = g_ref.shape
    positions = lax.axis_index("cp") * rows + lax.broadcasted_iota(jnp.int32, (8, rows), 1)

    def step(doc, carry):
        end, first = carry
        end = end + doc_ref[doc]
        return (end, jnp.where(end <= positions, end, first))

    _, first = lax.fori_loop(0, doc_ref.shape[0], step, (jnp.int32(0), jnp.zeros((8, rows), jnp.int32)))
    start_ref[...] = first
    for head in range(width // HD):
        cols = slice(head * HD, (head + 1) * HD)
        product = g_ref[:, cols].astype(jnp.float32) * o_ref[:, cols].astype(jnp.float32)
        delta_ref[head : head + 1, :] = jnp.sum(product.T, axis=0, keepdims=True)


def stats_entries(key_blocks, bits, kv_ref, q_ref, start_ref, m_ref, l_ref, bias_ref):
    heads = m_ref.shape[0]

    def step(i, carry):
        key = pick(key_blocks, i)

        @pl.when(listed(bits, key))
        def _():
            write_bias(bias_ref, start_ref, key)
            keys = kv_ref[i, 0]

            def products(head):
                return nt_dot(keys, q_ref[:, head * HD : (head + 1) * HD])

            ahead = products(0)
            for head in range(heads):
                scores = ahead * SCORE_SCALE + bias_ref[...]
                if head + 1 < heads:
                    ahead = products(head + 1)
                row = slice(head, head + 1)
                old_max = m_ref[row, :]
                new_max = jnp.maximum(old_max, jnp.max(scores, axis=0, keepdims=True))
                total = jnp.sum(jnp.exp2(scores - new_max), axis=0, keepdims=True)
                l_ref[row, :] = l_ref[row, :] * jnp.exp2(old_max - new_max) + total
                m_ref[row, :] = new_max

        return carry

    lax.fori_loop(0, len(key_blocks), step, 0)


def stats_own_kernel(q_ref, off_ref, start_ref, kv0, m_ref, l_ref, bias_ref, kv_ref):
    m_ref[...] = jnp.full_like(m_ref, EMPTY)
    l_ref[...] = jnp.zeros_like(l_ref)
    kv_ref[0] = kv0[1]
    kv_ref[1] = kv0[0]
    keys = [key_block(0, 0), key_block(0, 1)]
    stats_entries(keys, listed_bits(off_ref), kv_ref, q_ref, start_ref, m_ref, l_ref, bias_ref)


def stats_mid_kernel(q_ref, off_ref, start_ref, m_in, l_in, kv12, m_ref, l_ref, bias_ref, kv_ref):
    m_ref[...] = m_in[...]
    l_ref[...] = l_in[...]
    for i in range(4):
        kv_ref[i] = kv12[1 - i % 2, i // 2]
    keys = [key_block(1, i) for i in range(4)]
    stats_entries(keys, listed_bits(off_ref), kv_ref, q_ref, start_ref, m_ref, l_ref, bias_ref)


def grad_entries(key_blocks, bits, kv_ref, q_ref, g_ref, start_ref, lse_ref, delta_ref, dq_ref, bias_ref, part_ref):
    heads = lse_ref.shape[0]
    part_ref[...] = jnp.zeros_like(part_ref)

    def step(i, carry):
        key = pick(key_blocks, i)

        @pl.when(listed(bits, key))
        def _():
            write_bias(bias_ref, start_ref, key)
            keys = kv_ref[i, 0]
            values = kv_ref[i, 1]
            keys_t = keys.T

            def q_head(head):
                return q_ref[:, head * HD : (head + 1) * HD]

            def g_head(head):
                return g_ref[:, head * HD : (head + 1) * HD]

            def products(head):
                return nt_dot(keys, q_head(head)), nt_dot(values, g_head(head))

            def weights(head, ahead):
                row = slice(head, head + 1)
                probs = jnp.exp2(ahead[0] * SCORE_SCALE + bias_ref[...] - lse_ref[row, :])
                d_score = probs * (ahead[1] - delta_ref[row, :])
                return probs.astype(jnp.bfloat16), d_score.astype(jnp.bfloat16)

            def sums(head, pair, acc):
                at = head * HD
                dq_ref[at : at + HD, :] += nn_dot(keys_t, pair[1])
                d_key = nn_dot(pair[1], q_head(head))
                d_value = nn_dot(pair[0], g_head(head))
                return (d_key, d_value) if acc is None else (acc[0] + d_key, acc[1] + d_value)

            acc = None
            ahead, pair = products(0), None
            for head in range(heads):
                following = products(head + 1) if head + 1 < heads else None
                if pair is not None:
                    acc = sums(head - 1, pair, acc)
                pair, ahead = weights(head, ahead), following
            acc = sums(heads - 1, pair, acc)
            part_ref[i, :, 0:HD] = acc[0] * FACTOR
            part_ref[i, :, HD:] = acc[1]

        return carry

    lax.fori_loop(0, len(key_blocks), step, 0)


def grad_far_kernel(q_ref, g_ref, off_ref, start_ref, delta_ref, m_in, l_in, kv0, kv3, kv4,
                    p3_own, p_other, p4_ref, dq_ref, lse_ref, m_ref, l_ref, bias_ref, kv_ref, part_ref):
    core = core_parity()
    bits = listed_bits(off_ref)
    m_ref[...] = m_in[...]
    l_ref[...] = l_in[...]
    kv_ref[0] = kv3[1]
    kv_ref[1] = kv3[0]
    kv_ref[2] = kv4[...]
    kv_ref[3] = kv0[0]
    far = [key_block(3, 0), key_block(3, 1), key_block(3, 2)]
    stats_entries(far, bits, kv_ref, q_ref, start_ref, m_ref, l_ref, bias_ref)
    lse_ref[...] = m_ref[...] + jnp.log2(l_ref[...])
    dq_ref[...] = jnp.zeros_like(dq_ref)
    bits = jnp.where(core == 1, bits, bits & -2)
    keys = far + [key_block(0, 1)]
    grad_entries(keys, bits, kv_ref, q_ref, g_ref, start_ref, lse_ref, delta_ref, dq_ref, bias_ref, part_ref)
    p3_own[...] = part_ref[1 - core]
    p_other[0] = part_ref[core].astype(p_other.dtype)
    p_other[1] = part_ref[3].astype(p_other.dtype)
    p4_ref[...] = part_ref[2].astype(p4_ref.dtype)


def grad_mid_kernel(q_ref, g_ref, off_ref, start_ref, delta_ref, lse_ref, kv12, dq_in,
                    p_own, p_other, dq_ref, bias_ref, kv_ref, part_ref):
    for i in range(4):
        kv_ref[i] = kv12[1 - i % 2, i // 2]
    dq_ref[...] = dq_in[...]
    keys = [key_block(1, i) for i in range(4)]
    bits = listed_bits(off_ref)
    grad_entries(keys, bits, kv_ref, q_ref, g_ref, start_ref, lse_ref, delta_ref, dq_ref, bias_ref, part_ref)
    core = core_parity()
    for i in range(2):
        p_own[i] = part_ref[2 * i + 1 - core]
        p_other[i] = part_ref[2 * i + core].astype(p_other.dtype)


def grad_own_kernel(q_ref, g_ref, off_ref, start_ref, delta_ref, lse_ref, kv_in, dq_in,
                    p_own, out_ref, bias_ref, kv_ref, part_ref, dq_ref):
    kv_ref[0] = kv_in[...]
    dq_ref[...] = dq_in[...]
    keys = [lax.axis_index("cp")]
    bits = listed_bits(off_ref)
    grad_entries(keys, bits, kv_ref, q_ref, g_ref, start_ref, lse_ref, delta_ref, dq_ref, bias_ref, part_ref)
    p_own[...] = part_ref[0]
    for head in range(lse_ref.shape[0]):
        at = slice(head * HD, (head + 1) * HD)
        out_ref[:, at] = (dq_ref[at, :] * FACTOR).T.astype(out_ref.dtype)


def merge_far_kernel(own_ref, gathered_ref, out_ref):
    total = own_ref[...] + gathered_ref[1 - core_parity(), 0].astype(jnp.float32)
    out_ref[...] = total.astype(out_ref.dtype)


def merge_mid_kernel(own_ref, gathered_ref, back3_ref, back4_ref, p1_ref, p2_ref):
    other = gathered_ref.at[1 - core_parity()]
    p1_ref[...] = (own_ref[0] + other[0].astype(jnp.float32)).astype(p1_ref.dtype)
    total = own_ref[1] + other[1].astype(jnp.float32)
    total += back3_ref[...].astype(jnp.float32) + back4_ref[...].astype(jnp.float32)
    p2_ref[...] = total.astype(p2_ref.dtype)


def final_kernel(own_ref, gathered_ref, back2_ref, back1_ref, dk_ref, dv_ref):
    total = own_ref[...] + gathered_ref[1 - core_parity(), 1].astype(jnp.float32)
    total += back1_ref[...].astype(jnp.float32) + back2_ref[...].astype(jnp.float32)
    dk_ref[...] = total[:, 0:HD].astype(dk_ref.dtype)
    dv_ref[...] = total[:, HD:].astype(dv_ref.dtype)


def call(kernel, outs, scratch, units, *args, smem_args=0):
    pair = 2 * 8 * 256 * 256
    moved = sum(a.size * a.dtype.itemsize for a in args) + sum(o.size * o.dtype.itemsize for o in outs)
    spaces = [pltpu.SMEM] * smem_args + [pltpu.VMEM] * (len(args) - smem_args)
    return pl.pallas_call(
        kernel,
        out_shape=outs,
        in_specs=[pl.BlockSpec(memory_space=space) for space in spaces],
        out_specs=[pl.BlockSpec(memory_space=pltpu.VMEM) for _ in outs],
        scratch_shapes=scratch,
        compiler_params=pltpu.CompilerParams(vmem_limit_bytes=VMEM_BYTES),
        cost_estimate=pl.CostEstimate(flops=units * pair * HD, bytes_accessed=moved, transcendentals=pair),
    )(*args)


def on_device(queries, keys, values, outputs, out_grad, doc_lengths, block_offsets):
    rows, width = queries.shape
    heads = width // HD
    struct = jax.ShapeDtypeStruct
    f32, bf16 = jnp.float32, jnp.bfloat16
    stat = struct((heads, rows), f32)
    piece16, piece32 = struct((rows, 2 * HD), bf16), struct((rows, 2 * HD), f32)
    dq_part = struct((width, rows), f32)
    bias = pltpu.VMEM((rows, rows), f32)
    row_stat = pltpu.VMEM((heads, rows), f32)

    def stack(count):
        return pltpu.VMEM((count, 2, rows, HD), bf16)

    def parts(count):
        return pltpu.VMEM((count, rows, 2 * HD), f32)

    which = lax.broadcasted_iota(jnp.int32, (2, rows, HD), 0)
    kv = jnp.where(which == 0, keys[None], values[None])
    kv = lax.optimization_barrier(kv)
    kv2 = shift(kv, 4)
    both0 = gather_pair(kv)
    start, delta = call(
        prep_kernel, [struct((8, rows), jnp.int32), stat], [], 1, doc_lengths, out_grad, outputs, smem_args=1)
    m, l = call(
        stats_own_kernel, [stat, stat], [bias, stack(2)], 2, queries, block_offsets, start, both0)
    kv, m, l, delta = lax.optimization_barrier((kv, m, l, delta))
    kv1 = shift(kv, 2)
    kv2, m, l, delta = lax.optimization_barrier((kv2, m, l, delta))
    kv3 = shift(kv2, 2)
    kv4 = shift(kv2, 3, 1)
    both12 = gather_pair(jnp.stack([kv1, kv2]))
    m, l = call(
        stats_mid_kernel, [stat, stat], [bias, stack(4)], 4, queries, block_offsets, start, m, l, both12)
    both3 = gather_pair(kv3)

    known = (queries, out_grad, block_offsets, start, delta)
    pair16 = struct((2, rows, 2 * HD), bf16)
    p3_own, far_other, p4, dq, lse = call(
        grad_far_kernel, [piece32, pair16, piece16, dq_part, stat], [row_stat, row_stat, bias, stack(4), parts(4)],
        20, *known, m, l, both0, both3, kv4)
    back4 = shift(p4, -3, 0)
    far_both = gather_pair(far_other)
    (p3,) = call(merge_far_kernel, [piece16], [], 0, p3_own, far_both)
    back3 = shift(p3, -2)
    p12_own, mid_other, dq = call(
        grad_mid_kernel, [struct((2, rows, 2 * HD), f32), pair16, dq_part],
        [bias, stack(4), parts(4)], 20, *known, lse, both12, dq)
    p1, p2 = call(merge_mid_kernel, [piece16, piece16], [], 0, p12_own, gather_pair(mid_other), back3, back4)
    back2 = shift(p2, -4)
    back1 = shift(p1, -2)
    p0_own, grad_queries = call(
        grad_own_kernel, [piece32, struct((rows, width), bf16)],
        [bias, stack(1), parts(1), pltpu.VMEM((width, rows), f32)], 5, *known, lse, kv, dq)
    piece = struct((rows, HD), bf16)
    grad_keys, grad_values = call(final_kernel, [piece, piece], [], 0, p0_own, far_both, back2, back1)
    return grad_queries, grad_keys, grad_values


def solution(mesh):
    tokens = P(("dp", "cp"), "hd")
    return jax.shard_map(
        on_device,
        mesh=mesh,
        in_specs=(tokens, tokens, tokens, tokens, tokens, P("dp"), P(("dp", "cp"), None)),
        out_specs=(tokens, tokens, tokens),
        check_vma=False,
    )
```

```python
import jax
import jax.numpy as jnp
from jax import lax
from jax.experimental import pallas as pl
from jax.experimental.pallas import tpu as pltpu
from jax.sharding import PartitionSpec as P

HD = 128
FACTOR = HD ** (-0.5)
SCORE_SCALE = FACTOR * 1.4426950408889634
MASKED = -1e30
EMPTY = -1e20
VMEM_BYTES = 32 * 1024 * 1024


def shift(array, by, parity=None):
    n = lax.axis_size("cp")
    pairs = [(i, (i + by) % n) for i in range(n) if parity is None or i % 2 == parity]
    return lax.ppermute(array, "cp", pairs)


def gather_pair(array):
    n = lax.axis_size("cp")
    return lax.all_gather(array, "cp", axis_index_groups=[[i, i + 1] for i in range(0, n, 2)])


def nt_dot(a, b):
    return lax.dot_general(a, b, (((1,), (1,)), ((), ())), preferred_element_type=jnp.float32)


def nn_dot(a, b):
    return lax.dot_general(a, b, (((1,), (0,)), ((), ())), preferred_element_type=jnp.float32)


def core_parity():
    return lax.rem(lax.axis_index("cp"), 2)


def key_block(slot, entry):
    return lax.axis_index("cp") - core_parity() + 1 - 2 * slot - entry


def listed_bits(off_ref):
    offsets = off_ref[...]
    bits = jnp.where(offsets >= 0, lax.shift_left(jnp.ones_like(offsets), jnp.maximum(offsets, 0)), 0)
    return jnp.sum(bits.astype(jnp.float32)).astype(jnp.int32)


def pick(values, i):
    chosen = values[0]
    for j in range(1, len(values)):
        chosen = jnp.where(i == j, values[j], chosen)
    return chosen


def listed(bits, key):
    block = lax.axis_index("cp")
    bit = lax.shift_right_logical(bits, jnp.maximum(block - key, 0)) & 1
    return (bit == 1) & (block >= key) & (key >= 0)


def write_bias(bias_ref, start_ref, key):
    rows = bias_ref.shape[0]
    key_pos = key * rows + lax.broadcasted_iota(jnp.int32, bias_ref.shape, 0)
    q_pos = lax.axis_index("cp") * rows + lax.broadcasted_iota(jnp.int32, bias_ref.shape, 1)
    allowed = (key_pos >= start_ref[0:1, :]) & (key_pos <= q_pos)
    bias_ref[...] = jnp.where(allowed, 0.0, MASKED)


def prep_kernel(doc_ref, g_ref, o_ref, start_ref, delta_ref):
    rows, width = g_ref.shape
    positions = lax.axis_index("cp") * rows + lax.broadcasted_iota(jnp.int32, (8, rows), 1)

    def step(doc, carry):
        end, first = carry
        end = end + doc_ref[doc]
        return (end, jnp.where(end <= positions, end, first))

    _, first = lax.fori_loop(0, doc_ref.shape[0], step, (jnp.int32(0), jnp.zeros((8, rows), jnp.int32)))
    start_ref[...] = first
    for head in range(width // HD):
        cols = slice(head * HD, (head + 1) * HD)
        product = g_ref[:, cols].astype(jnp.float32) * o_ref[:, cols].astype(jnp.float32)
        delta_ref[head : head + 1, :] = jnp.sum(product.T, axis=0, keepdims=True)


def stats_entries(key_blocks, bits, kv_ref, q_ref, start_ref, m_ref, l_ref, bias_ref):
    heads = m_ref.shape[0]

    def step(i, carry):
        key = pick(key_blocks, i)

        @pl.when(listed(bits, key))
        def _():
            write_bias(bias_ref, start_ref, key)
            keys = kv_ref[i, 0]

            def products(head):
                return nt_dot(keys, q_ref[:, head * HD : (head + 1) * HD])

            ahead = products(0)
            for head in range(heads):
                scores = ahead * SCORE_SCALE + bias_ref[...]
                if head + 1 < heads:
                    ahead = products(head + 1)
                row = slice(head, head + 1)
                old_max = m_ref[row, :]
                new_max = jnp.maximum(old_max, jnp.max(scores, axis=0, keepdims=True))
                total = jnp.sum(jnp.exp2(scores - new_max), axis=0, keepdims=True)
                l_ref[row, :] = l_ref[row, :] * jnp.exp2(old_max - new_max) + total
                m_ref[row, :] = new_max

        return carry

    lax.fori_loop(0, len(key_blocks), step, 0)


def stats_own_kernel(q_ref, off_ref, start_ref, kv0, m_ref, l_ref, bias_ref, kv_ref):
    m_ref[...] = jnp.full_like(m_ref, EMPTY)
    l_ref[...] = jnp.zeros_like(l_ref)
    kv_ref[0] = kv0[1]
    kv_ref[1] = kv0[0]
    keys = [key_block(0, 0), key_block(0, 1)]
    stats_entries(keys, listed_bits(off_ref), kv_ref, q_ref, start_ref, m_ref, l_ref, bias_ref)


def stats_mid_kernel(q_ref, off_ref, start_ref, m_in, l_in, kv12, m_ref, l_ref, bias_ref, kv_ref):
    m_ref[...] = m_in[...]
    l_ref[...] = l_in[...]
    for i in range(4):
        kv_ref[i] = kv12[1 - i % 2, i // 2]
    keys = [key_block(1, i) for i in range(4)]
    stats_entries(keys, listed_bits(off_ref), kv_ref, q_ref, start_ref, m_ref, l_ref, bias_ref)


def grad_entries(key_blocks, bits, kv_ref, q_ref, g_ref, start_ref, lse_ref, delta_ref, dq_ref, bias_ref, part_ref):
    heads = lse_ref.shape[0]
    def step(i, carry):
        key = pick(key_blocks, i)
        present = listed(bits, key)

        @pl.when(jnp.logical_not(present))
        def _():
            part_ref[i] = jnp.zeros(part_ref.shape[1:], part_ref.dtype)

        @pl.when(present)
        def _():
            write_bias(bias_ref, start_ref, key)
            keys = kv_ref[i, 0]
            values = kv_ref[i, 1]
            keys_t = keys.T

            def q_head(head):
                return q_ref[:, head * HD : (head + 1) * HD]

            def g_head(head):
                return g_ref[:, head * HD : (head + 1) * HD]

            def products(head):
                return nt_dot(keys, q_head(head)), nt_dot(values, g_head(head))

            def weights(head, ahead):
                row = slice(head, head + 1)
                probs = jnp.exp2(ahead[0] * SCORE_SCALE + bias_ref[...] - lse_ref[row, :])
                d_score = probs * (ahead[1] - delta_ref[row, :])
                return probs.astype(jnp.bfloat16), d_score.astype(jnp.bfloat16)

            def sums(head, pair, acc):
                at = head * HD
                dq_ref[at : at + HD, :] += nn_dot(keys_t, pair[1])
                d_key = nn_dot(pair[1], q_head(head))
                d_value = nn_dot(pair[0], g_head(head))
                return (d_key, d_value) if acc is None else (acc[0] + d_key, acc[1] + d_value)

            acc = None
            ahead, pair = products(0), None
            for head in range(heads):
                following = products(head + 1) if head + 1 < heads else None
                if pair is not None:
                    acc = sums(head - 1, pair, acc)
                pair, ahead = weights(head, ahead), following
            acc = sums(heads - 1, pair, acc)
            part_ref[i, :, 0:HD] = acc[0] * FACTOR
            part_ref[i, :, HD:] = acc[1]

        return carry

    lax.fori_loop(0, len(key_blocks), step, 0)


def grad_far_kernel(q_ref, g_ref, off_ref, start_ref, delta_ref, m_in, l_in, kv0, kv3, kv4,
                    p3_own, p_other, p4_ref, dq_ref, lse_ref, m_ref, l_ref, bias_ref, kv_ref, part_ref):
    core = core_parity()
    bits = listed_bits(off_ref)
    m_ref[...] = m_in[...]
    l_ref[...] = l_in[...]
    kv_ref[0] = kv3[1]
    kv_ref[1] = kv3[0]
    kv_ref[2] = kv4[...]
    kv_ref[3] = kv0[0]
    far = [key_block(3, 0), key_block(3, 1), key_block(3, 2)]
    stats_entries(far, bits, kv_ref, q_ref, start_ref, m_ref, l_ref, bias_ref)
    lse_ref[...] = m_ref[...] + jnp.log2(l_ref[...])
    dq_ref[...] = jnp.zeros_like(dq_ref)
    bits = jnp.where(core == 1, bits, bits & -2)
    keys = far + [key_block(0, 1)]
    grad_entries(keys, bits, kv_ref, q_ref, g_ref, start_ref, lse_ref, delta_ref, dq_ref, bias_ref, part_ref)
    p3_own[...] = part_ref[1 - core]
    p_other[0] = part_ref[core].astype(p_other.dtype)
    p_other[1] = part_ref[3].astype(p_other.dtype)
    p4_ref[...] = part_ref[2].astype(p4_ref.dtype)


def grad_mid_kernel(q_ref, g_ref, off_ref, start_ref, delta_ref, lse_ref, kv12, dq_in,
                    p2_own, p_other, dq_ref, bias_ref, kv_ref, part_ref):
    del dq_in
    core = core_parity()
    kv_ref[0] = kv12[1, 1]
    kv_ref[1] = kv12[0, 1]
    kv_ref[2] = kv12[1 - core, 0]
    keys = [key_block(2, 0), key_block(2, 1), key_block(1, core)]
    bits = listed_bits(off_ref)
    grad_entries(keys, bits, kv_ref, q_ref, g_ref, start_ref, lse_ref, delta_ref, dq_ref, bias_ref, part_ref)
    p2_own[...] = part_ref[1 - core]
    p_other[0] = part_ref[2].astype(p_other.dtype)
    p_other[1] = part_ref[core].astype(p_other.dtype)


def grad_near_kernel(q_ref, g_ref, off_ref, start_ref, delta_ref, lse_ref, kv_in, gathered_ref, dq_in,
                     p1_ref, dq_ref, bias_ref, kv_ref, part_ref):
    del dq_in
    core = core_parity()
    kv_ref[0] = kv_in[...]
    keys = [key_block(1, 1 - core)]
    bits = listed_bits(off_ref)
    grad_entries(keys, bits, kv_ref, q_ref, g_ref, start_ref, lse_ref, delta_ref, dq_ref, bias_ref, part_ref)
    p1_ref[...] = (part_ref[0] + gathered_ref[1 - core, 0].astype(jnp.float32)).astype(p1_ref.dtype)


def grad_own_kernel(q_ref, g_ref, off_ref, start_ref, delta_ref, lse_ref, kv_in, dq_in,
                    p_own, out_ref, bias_ref, kv_ref, part_ref, dq_ref):
    kv_ref[0] = kv_in[...]
    dq_ref[...] = dq_in[...]
    keys = [lax.axis_index("cp")]
    bits = listed_bits(off_ref)
    grad_entries(keys, bits, kv_ref, q_ref, g_ref, start_ref, lse_ref, delta_ref, dq_ref, bias_ref, part_ref)
    p_own[...] = part_ref[0]
    for head in range(lse_ref.shape[0]):
        at = slice(head * HD, (head + 1) * HD)
        out_ref[:, at] = (dq_ref[at, :] * FACTOR).T.astype(out_ref.dtype)


def merge_far_kernel(own_ref, gathered_ref, out_ref):
    total = own_ref[...] + gathered_ref[1 - core_parity(), 0].astype(jnp.float32)
    out_ref[...] = total.astype(out_ref.dtype)


def merge_mid_kernel(own_ref, gathered_ref, back3_ref, back4_ref, p2_ref):
    total = own_ref[...] + gathered_ref[1 - core_parity(), 1].astype(jnp.float32)
    total += back3_ref[...].astype(jnp.float32) + back4_ref[...].astype(jnp.float32)
    p2_ref[...] = total.astype(p2_ref.dtype)


def final_kernel(own_ref, gathered_ref, back1_ref, dk_ref, dv_ref):
    total = own_ref[...] + gathered_ref[1 - core_parity(), 1].astype(jnp.float32)
    total += back1_ref[...].astype(jnp.float32)
    dk_ref[...] = total[:, 0:HD].astype(dk_ref.dtype)
    dv_ref[...] = total[:, HD:].astype(dv_ref.dtype)


def call(kernel, outs, scratch, units, *args, smem_args=0, aliases=None):
    pair = 2 * 8 * 256 * 256
    moved = sum(a.size * a.dtype.itemsize for a in args) + sum(o.size * o.dtype.itemsize for o in outs)
    spaces = [pltpu.SMEM] * smem_args + [pltpu.VMEM] * (len(args) - smem_args)
    return pl.pallas_call(
        kernel,
        out_shape=outs,
        in_specs=[pl.BlockSpec(memory_space=space) for space in spaces],
        out_specs=[pl.BlockSpec(memory_space=pltpu.VMEM) for _ in outs],
        scratch_shapes=scratch,
        input_output_aliases=aliases or {},
        compiler_params=pltpu.CompilerParams(vmem_limit_bytes=VMEM_BYTES),
        cost_estimate=pl.CostEstimate(flops=units * pair * HD, bytes_accessed=moved, transcendentals=pair),
    )(*args)


def on_device(queries, keys, values, outputs, out_grad, doc_lengths, block_offsets):
    rows, width = queries.shape
    heads = width // HD
    struct = jax.ShapeDtypeStruct
    f32, bf16 = jnp.float32, jnp.bfloat16
    stat = struct((heads, rows), f32)
    piece16, piece32 = struct((rows, 2 * HD), bf16), struct((rows, 2 * HD), f32)
    dq_part = struct((width, rows), f32)
    bias = pltpu.VMEM((rows, rows), f32)
    row_stat = pltpu.VMEM((heads, rows), f32)

    def stack(count):
        return pltpu.VMEM((count, 2, rows, HD), bf16)

    def parts(count):
        return pltpu.VMEM((count, rows, 2 * HD), f32)

    which = lax.broadcasted_iota(jnp.int32, (2, rows, HD), 0)
    kv = jnp.where(which == 0, keys[None], values[None])
    kv = lax.optimization_barrier(kv)
    kv2 = shift(kv, 4)
    both0 = gather_pair(kv)
    start, delta = call(
        prep_kernel, [struct((8, rows), jnp.int32), stat], [], 1, doc_lengths, out_grad, outputs, smem_args=1)
    m, l = call(
        stats_own_kernel, [stat, stat], [bias, stack(2)], 2, queries, block_offsets, start, both0)
    kv, m, l, delta = lax.optimization_barrier((kv, m, l, delta))
    kv1 = shift(kv, 2)
    kv2, m, l, delta = lax.optimization_barrier((kv2, m, l, delta))
    kv3 = shift(kv2, 2)
    kv4 = shift(kv2, 3, 1)
    both12 = gather_pair(jnp.stack([kv1, kv2]))
    m, l = call(
        stats_mid_kernel, [stat, stat], [bias, stack(4)], 4, queries, block_offsets, start, m, l, both12)
    both3 = gather_pair(kv3)

    known = (queries, out_grad, block_offsets, start, delta)
    pair16 = struct((2, rows, 2 * HD), bf16)
    p3_own, far_other, p4, dq, lse = call(
        grad_far_kernel, [piece32, pair16, piece16, dq_part, stat], [row_stat, row_stat, bias, stack(4), parts(4)],
        20, *known, m, l, both0, both3, kv4)
    back4 = shift(p4, -3, 0)
    far_both = gather_pair(far_other)
    (p3,) = call(merge_far_kernel, [piece16], [], 0, p3_own, far_both)
    back3 = shift(p3, -2)
    p2_own, mid_other, dq = call(
        grad_mid_kernel, [piece32, pair16, dq_part], [bias, stack(3), parts(3)], 15,
        *known, lse, both12, dq, aliases={7: 2})
    mid_both = gather_pair(mid_other)
    (p2,) = call(merge_mid_kernel, [piece16], [], 0, p2_own, mid_both, back3, back4)
    back2 = shift(p2, -4)
    p1, dq = call(
        grad_near_kernel, [piece16, dq_part], [bias, stack(1), parts(1)], 5,
        *known, lse, kv1, mid_both, dq, aliases={8: 1})
    back1 = shift(p1, -2)
    p0_own, grad_queries = call(
        grad_own_kernel, [piece32, struct((rows, width), bf16)],
        [bias, stack(1), parts(1), pltpu.VMEM((width, rows), f32)], 5, *known, lse, kv, dq)
    piece = struct((rows, HD), bf16)
    grad_keys, grad_values = call(final_kernel, [piece, piece], [], 0, p0_own + back2.astype(f32), far_both, back1)
    return grad_queries, grad_keys, grad_values


def solution(mesh):
    tokens = P(("dp", "cp"), "hd")
    return jax.shard_map(
        on_device,
        mesh=mesh,
        in_specs=(tokens, tokens, tokens, tokens, tokens, P("dp"), P(("dp", "cp"), None)),
        out_specs=(tokens, tokens, tokens),
        check_vma=False,
    )
```

```python
import jax
import jax.numpy as jnp
from jax import lax
from jax.experimental import pallas as pl
from jax.experimental.pallas import tpu as pltpu
from jax.sharding import PartitionSpec as P

HD = 128
FACTOR = HD ** (-0.5)
SCORE_SCALE = FACTOR * 1.4426950408889634
MASKED = -1e30
EMPTY = -1e20
VMEM_BYTES = 32 * 1024 * 1024


def shift(array, by, parity=None):
    n = lax.axis_size("cp")
    pairs = [(i, i + by) for i in range(n) if 0 <= i + by < n and parity in (None, i % 2)]
    return lax.ppermute(array, "cp", pairs)


def gather_pair(array):
    n = lax.axis_size("cp")
    return lax.all_gather(array, "cp", axis_index_groups=[[i, i + 1] for i in range(0, n, 2)])


def nt_dot(a, b):
    return lax.dot_general(a, b, (((1,), (1,)), ((), ())), preferred_element_type=jnp.float32)


def nn_dot(a, b):
    return lax.dot_general(a, b, (((1,), (0,)), ((), ())), preferred_element_type=jnp.float32)


def core_parity():
    return lax.rem(lax.axis_index("cp"), 2)


def key_block(slot, entry):
    return lax.axis_index("cp") - core_parity() + 1 - 2 * slot - entry


def listed_bits(off_ref):
    offsets = off_ref[...]
    bits = jnp.where(offsets >= 0, lax.shift_left(jnp.ones_like(offsets), jnp.maximum(offsets, 0)), 0)
    return jnp.sum(bits.astype(jnp.float32)).astype(jnp.int32)


def pick(values, i):
    chosen = values[0]
    for j in range(1, len(values)):
        chosen = jnp.where(i == j, values[j], chosen)
    return chosen


def listed(bits, key):
    block = lax.axis_index("cp")
    bit = lax.shift_right_logical(bits, jnp.maximum(block - key, 0)) & 1
    return (bit == 1) & (block >= key) & (key >= 0)


def write_bias(bias_ref, start_ref, key):
    rows = bias_ref.shape[0]
    key_pos = key * rows + lax.broadcasted_iota(jnp.int32, bias_ref.shape, 0)
    q_pos = lax.axis_index("cp") * rows + lax.broadcasted_iota(jnp.int32, bias_ref.shape, 1)
    allowed = (key_pos >= start_ref[0:1, :]) & (key_pos <= q_pos)
    bias_ref[...] = jnp.where(allowed, 0.0, MASKED)


def prep_kernel(doc_ref, g_ref, o_ref, start_ref, delta_ref):
    rows, width = g_ref.shape
    positions = lax.axis_index("cp") * rows + lax.broadcasted_iota(jnp.int32, (8, rows), 1)

    def step(doc, carry):
        end, first = carry
        end = end + doc_ref[doc]
        return (end, jnp.where(end <= positions, end, first))

    _, first = lax.fori_loop(0, doc_ref.shape[0], step, (jnp.int32(0), jnp.zeros((8, rows), jnp.int32)))
    start_ref[...] = first
    for head in range(width // HD):
        cols = slice(head * HD, (head + 1) * HD)
        product = g_ref[:, cols].astype(jnp.float32) * o_ref[:, cols].astype(jnp.float32)
        delta_ref[head : head + 1, :] = jnp.sum(product.T, axis=0, keepdims=True)


def stats_entries(key_blocks, bits, kv_ref, q_ref, start_ref, m_ref, l_ref, bias_ref):
    heads = m_ref.shape[0]

    def step(i, carry):
        key = pick(key_blocks, i)

        @pl.when(listed(bits, key))
        def _():
            write_bias(bias_ref, start_ref, key)
            keys = kv_ref[i, 0]

            def products(head):
                return nt_dot(keys, q_ref[:, head * HD : (head + 1) * HD])

            ahead = products(0)
            for head in range(heads):
                scores = ahead * SCORE_SCALE + bias_ref[...]
                if head + 1 < heads:
                    ahead = products(head + 1)
                row = slice(head, head + 1)
                old_max = m_ref[row, :]
                new_max = jnp.maximum(old_max, jnp.max(scores, axis=0, keepdims=True))
                total = jnp.sum(jnp.exp2(scores - new_max), axis=0, keepdims=True)
                l_ref[row, :] = l_ref[row, :] * jnp.exp2(old_max - new_max) + total
                m_ref[row, :] = new_max

        return carry

    lax.fori_loop(0, len(key_blocks), step, 0)


def stats_own_kernel(q_ref, off_ref, start_ref, kv0, m_ref, l_ref, bias_ref, kv_ref):
    m_ref[...] = jnp.full_like(m_ref, EMPTY)
    l_ref[...] = jnp.zeros_like(l_ref)
    kv_ref[0] = kv0[1]
    kv_ref[1] = kv0[0]
    keys = [key_block(0, 0), key_block(0, 1)]
    stats_entries(keys, listed_bits(off_ref), kv_ref, q_ref, start_ref, m_ref, l_ref, bias_ref)


def stats_mid_kernel(q_ref, off_ref, start_ref, m_in, l_in, kv12, m_ref, l_ref, bias_ref, kv_ref):
    m_ref[...] = m_in[...]
    l_ref[...] = l_in[...]
    for i in range(4):
        kv_ref[i] = kv12[1 - i % 2, i // 2]
    keys = [key_block(1, i) for i in range(4)]
    stats_entries(keys, listed_bits(off_ref), kv_ref, q_ref, start_ref, m_ref, l_ref, bias_ref)


def grad_entries(key_blocks, bits, kv_ref, q_ref, g_ref, start_ref, lse_ref, delta_ref, dq_ref, bias_ref, part_ref):
    heads = lse_ref.shape[0]
    def step(i, carry):
        key = pick(key_blocks, i)
        present = listed(bits, key)

        @pl.when(jnp.logical_not(present))
        def _():
            part_ref[i] = jnp.zeros(part_ref.shape[1:], part_ref.dtype)

        @pl.when(present)
        def _():
            write_bias(bias_ref, start_ref, key)
            keys = kv_ref[i, 0]
            values = kv_ref[i, 1]
            keys_t = keys.T

            def q_head(head):
                return q_ref[:, head * HD : (head + 1) * HD]

            def g_head(head):
                return g_ref[:, head * HD : (head + 1) * HD]

            def products(head):
                return nt_dot(keys, q_head(head)), nt_dot(values, g_head(head))

            def weights(head, ahead):
                row = slice(head, head + 1)
                probs = jnp.exp2(ahead[0] * SCORE_SCALE + bias_ref[...] - lse_ref[row, :])
                d_score = probs * (ahead[1] - delta_ref[row, :])
                return probs.astype(jnp.bfloat16), d_score.astype(jnp.bfloat16)

            def sums(head, pair, acc):
                at = head * HD
                dq_ref[at : at + HD, :] += nn_dot(keys_t, pair[1])
                d_key = nn_dot(pair[1], q_head(head))
                d_value = nn_dot(pair[0], g_head(head))
                return (d_key, d_value) if acc is None else (acc[0] + d_key, acc[1] + d_value)

            acc = None
            ahead, pair = products(0), None
            for head in range(heads):
                following = products(head + 1) if head + 1 < heads else None
                if pair is not None:
                    acc = sums(head - 1, pair, acc)
                pair, ahead = weights(head, ahead), following
            acc = sums(heads - 1, pair, acc)
            part_ref[i, :, 0:HD] = acc[0] * FACTOR
            part_ref[i, :, HD:] = acc[1]

        return carry

    lax.fori_loop(0, len(key_blocks), step, 0)


def grad_far_kernel(q_ref, g_ref, off_ref, start_ref, delta_ref, m_in, l_in, kv0, kv3, kv4,
                    p3_own, p_other, p4_ref, dq_ref, lse_ref, m_ref, l_ref, bias_ref, kv_ref, part_ref):
    core = core_parity()
    bits = listed_bits(off_ref)
    m_ref[...] = m_in[...]
    l_ref[...] = l_in[...]
    kv_ref[0] = kv3[1]
    kv_ref[1] = kv3[0]
    kv_ref[2] = kv4[...]
    kv_ref[3] = kv0[0]
    far = [key_block(3, 0), key_block(3, 1), key_block(3, 2)]
    stats_entries(far, bits, kv_ref, q_ref, start_ref, m_ref, l_ref, bias_ref)
    lse_ref[...] = m_ref[...] + jnp.log2(l_ref[...])
    dq_ref[...] = jnp.zeros_like(dq_ref)
    bits = jnp.where(core == 1, bits, bits & -2)
    keys = far + [key_block(0, 1)]
    grad_entries(keys, bits, kv_ref, q_ref, g_ref, start_ref, lse_ref, delta_ref, dq_ref, bias_ref, part_ref)
    p3_own[...] = part_ref[1 - core]
    p_other[0] = part_ref[core].astype(p_other.dtype)
    p_other[1] = part_ref[3].astype(p_other.dtype)
    p4_ref[...] = part_ref[2].astype(p4_ref.dtype)


def grad_mid_kernel(q_ref, g_ref, off_ref, start_ref, delta_ref, lse_ref, kv12, dq_in,
                    p2_own, p_other, dq_ref, bias_ref, kv_ref, part_ref):
    del dq_in
    core = core_parity()
    kv_ref[0] = kv12[1, 1]
    kv_ref[1] = kv12[0, 1]
    kv_ref[2] = kv12[1 - core, 0]
    keys = [key_block(2, 0), key_block(2, 1), key_block(1, core)]
    bits = listed_bits(off_ref)
    grad_entries(keys, bits, kv_ref, q_ref, g_ref, start_ref, lse_ref, delta_ref, dq_ref, bias_ref, part_ref)
    p2_own[...] = part_ref[1 - core]
    p_other[0] = part_ref[2].astype(p_other.dtype)
    p_other[1] = part_ref[core].astype(p_other.dtype)


def grad_near_kernel(q_ref, g_ref, off_ref, start_ref, delta_ref, lse_ref, kv_in, gathered_ref, dq_in,
                     p1_ref, dq_ref, bias_ref, kv_ref, part_ref):
    del dq_in
    core = core_parity()
    kv_ref[0] = kv_in[...]
    keys = [key_block(1, 1 - core)]
    bits = listed_bits(off_ref)
    grad_entries(keys, bits, kv_ref, q_ref, g_ref, start_ref, lse_ref, delta_ref, dq_ref, bias_ref, part_ref)
    p1_ref[...] = (part_ref[0] + gathered_ref[1 - core, 0].astype(jnp.float32)).astype(p1_ref.dtype)


def grad_own_kernel(q_ref, g_ref, off_ref, start_ref, delta_ref, lse_ref, kv_in, dq_in,
                    p_own, out_ref, bias_ref, kv_ref, part_ref, dq_ref):
    kv_ref[0] = kv_in[...]
    dq_ref[...] = dq_in[...]
    keys = [lax.axis_index("cp")]
    bits = listed_bits(off_ref)
    grad_entries(keys, bits, kv_ref, q_ref, g_ref, start_ref, lse_ref, delta_ref, dq_ref, bias_ref, part_ref)
    p_own[...] = part_ref[0]
    for head in range(lse_ref.shape[0]):
        at = slice(head * HD, (head + 1) * HD)
        out_ref[:, at] = (dq_ref[at, :] * FACTOR).T.astype(out_ref.dtype)


def merge_far_kernel(own_ref, gathered_ref, out_ref):
    total = own_ref[...] + gathered_ref[1 - core_parity(), 0].astype(jnp.float32)
    out_ref[...] = total.astype(out_ref.dtype)


def merge_mid_kernel(own_ref, gathered_ref, back3_ref, back4_ref, p2_ref):
    total = own_ref[...] + gathered_ref[1 - core_parity(), 1].astype(jnp.float32)
    total += back3_ref[...].astype(jnp.float32) + back4_ref[...].astype(jnp.float32)
    p2_ref[...] = total.astype(p2_ref.dtype)


def final_kernel(own_ref, gathered_ref, back1_ref, dk_ref, dv_ref):
    total = own_ref[...] + gathered_ref[1 - core_parity(), 1].astype(jnp.float32)
    total += back1_ref[...].astype(jnp.float32)
    dk_ref[...] = total[:, 0:HD].astype(dk_ref.dtype)
    dv_ref[...] = total[:, HD:].astype(dv_ref.dtype)


def call(kernel, outs, scratch, units, *args, smem_args=0, aliases=None):
    pair = 2 * 8 * 256 * 256
    moved = sum(a.size * a.dtype.itemsize for a in args) + sum(o.size * o.dtype.itemsize for o in outs)
    spaces = [pltpu.SMEM] * smem_args + [pltpu.VMEM] * (len(args) - smem_args)
    return pl.pallas_call(
        kernel,
        out_shape=outs,
        in_specs=[pl.BlockSpec(memory_space=space) for space in spaces],
        out_specs=[pl.BlockSpec(memory_space=pltpu.VMEM) for _ in outs],
        scratch_shapes=scratch,
        input_output_aliases=aliases or {},
        compiler_params=pltpu.CompilerParams(vmem_limit_bytes=VMEM_BYTES),
        cost_estimate=pl.CostEstimate(flops=units * pair * HD, bytes_accessed=moved, transcendentals=pair),
    )(*args)


def on_device(queries, keys, values, outputs, out_grad, doc_lengths, block_offsets):
    rows, width = queries.shape
    heads = width // HD
    struct = jax.ShapeDtypeStruct
    f32, bf16 = jnp.float32, jnp.bfloat16
    stat = struct((heads, rows), f32)
    piece16, piece32 = struct((rows, 2 * HD), bf16), struct((rows, 2 * HD), f32)
    dq_part = struct((width, rows), f32)
    bias = pltpu.VMEM((rows, rows), f32)
    row_stat = pltpu.VMEM((heads, rows), f32)

    def stack(count):
        return pltpu.VMEM((count, 2, rows, HD), bf16)

    def parts(count):
        return pltpu.VMEM((count, rows, 2 * HD), f32)

    which = lax.broadcasted_iota(jnp.int32, (2, rows, HD), 0)
    kv = jnp.where(which == 0, keys[None], values[None])
    kv = lax.optimization_barrier(kv)
    kv2 = shift(kv, 4)
    both0 = gather_pair(kv)
    start, delta = call(
        prep_kernel, [struct((8, rows), jnp.int32), stat], [], 1, doc_lengths, out_grad, outputs, smem_args=1)
    m, l = call(
        stats_own_kernel, [stat, stat], [bias, stack(2)], 2, queries, block_offsets, start, both0)
    kv, m, l, delta = lax.optimization_barrier((kv, m, l, delta))
    kv1 = shift(kv, 2)
    kv2, m, l, delta = lax.optimization_barrier((kv2, m, l, delta))
    kv3 = shift(kv2, 2)
    kv4 = shift(kv2, 3, 1)
    both12 = gather_pair(jnp.stack([kv1, kv2]))
    m, l = call(
        stats_mid_kernel, [stat, stat], [bias, stack(4)], 4, queries, block_offsets, start, m, l, both12)
    both3 = gather_pair(kv3)

    known = (queries, out_grad, block_offsets, start, delta)
    pair16 = struct((2, rows, 2 * HD), bf16)
    p3_own, far_other, p4, dq, lse = call(
        grad_far_kernel, [piece32, pair16, piece16, dq_part, stat], [row_stat, row_stat, bias, stack(4), parts(4)],
        20, *known, m, l, both0, both3, kv4)
    back4 = shift(p4, -3, 0)
    far_both = gather_pair(far_other)
    (p3,) = call(merge_far_kernel, [piece16], [], 0, p3_own, far_both)
    back3 = shift(p3, -2)
    p2_own, mid_other, dq = call(
        grad_mid_kernel, [piece32, pair16, dq_part], [bias, stack(3), parts(3)], 15,
        *known, lse, both12, dq, aliases={7: 2})
    mid_both = gather_pair(mid_other)
    (p2,) = call(merge_mid_kernel, [piece16], [], 0, p2_own, mid_both, back3, back4)
    back2 = shift(p2, -4)
    p1, dq = call(
        grad_near_kernel, [piece16, dq_part], [bias, stack(1), parts(1)], 5,
        *known, lse, kv1, mid_both, dq, aliases={8: 1})
    back1 = shift(p1, -2)
    p0_own, grad_queries = call(
        grad_own_kernel, [piece32, struct((rows, width), bf16)],
        [bias, stack(1), parts(1), pltpu.VMEM((width, rows), f32)], 5, *known, lse, kv, dq)
    piece = struct((rows, HD), bf16)
    grad_keys, grad_values = call(final_kernel, [piece, piece], [], 0, p0_own + back2.astype(f32), far_both, back1)
    return grad_queries, grad_keys, grad_values


def solution(mesh):
    tokens = P(("dp", "cp"), "hd")
    return jax.shard_map(
        on_device,
        mesh=mesh,
        in_specs=(tokens, tokens, tokens, tokens, tokens, P("dp"), P(("dp", "cp"), None)),
        out_specs=(tokens, tokens, tokens),
        check_vma=False,
    )
```

```python
import jax
import jax.numpy as jnp
from jax import lax
from jax.experimental import pallas as pl
from jax.experimental.pallas import tpu as pltpu
from jax.sharding import PartitionSpec as P

HD = 128
FACTOR = HD ** (-0.5)
SCORE_SCALE = FACTOR * 1.4426950408889634
MASKED = -1e30
EMPTY = -1e20
VMEM_BYTES = 32 * 1024 * 1024


def shift(array, by, parity=None):
    n = lax.axis_size("cp")
    pairs = [(i, i + by) for i in range(n) if 0 <= i + by < n and parity in (None, i % 2)]
    return lax.ppermute(array, "cp", pairs)


def gather_pair(array):
    n = lax.axis_size("cp")
    return lax.all_gather(array, "cp", axis_index_groups=[[i, i + 1] for i in range(0, n, 2)])


def nt_dot(a, b):
    return lax.dot_general(a, b, (((1,), (1,)), ((), ())), preferred_element_type=jnp.float32)


def nn_dot(a, b):
    return lax.dot_general(a, b, (((1,), (0,)), ((), ())), preferred_element_type=jnp.float32)


def core_parity():
    return lax.rem(lax.axis_index("cp"), 2)


def key_block(slot, entry):
    return lax.axis_index("cp") - core_parity() + 1 - 2 * slot - entry


def listed_bits(start_ref):
    return start_ref[1, 0]


def pick(values, i):
    chosen = values[0]
    for j in range(1, len(values)):
        chosen = jnp.where(i == j, values[j], chosen)
    return chosen


def listed(bits, key):
    block = lax.axis_index("cp")
    bit = lax.shift_right_logical(bits, jnp.maximum(block - key, 0)) & 1
    return (bit == 1) & (block >= key) & (key >= 0)


def write_bias(bias_ref, start_ref, key):
    rows = bias_ref.shape[0]
    key_pos = key * rows + lax.broadcasted_iota(jnp.int32, bias_ref.shape, 0)
    q_pos = lax.axis_index("cp") * rows + lax.broadcasted_iota(jnp.int32, bias_ref.shape, 1)
    allowed = (key_pos >= start_ref[0:1, :]) & (key_pos <= q_pos)
    bias_ref[...] = jnp.where(allowed, 0.0, MASKED)


def prep_kernel(doc_ref, off_ref, g_ref, o_ref, start_ref, delta_ref):
    rows, width = g_ref.shape
    positions = lax.axis_index("cp") * rows + lax.broadcasted_iota(jnp.int32, (8, rows), 1)

    def step(doc, carry):
        end, first = carry
        end = end + doc_ref[doc]
        return (end, jnp.where(end <= positions, end, first))

    _, first = lax.fori_loop(0, doc_ref.shape[0], step, (jnp.int32(0), jnp.zeros((8, rows), jnp.int32)))
    offsets = off_ref[...]
    listed_once = jnp.where(offsets >= 0, lax.shift_left(jnp.ones_like(offsets), jnp.maximum(offsets, 0)), 0)
    bits = jnp.sum(listed_once.astype(jnp.float32)).astype(jnp.int32)
    line = lax.broadcasted_iota(jnp.int32, first.shape, 0)
    start_ref[...] = jnp.where(line == 1, bits, first)
    for head in range(width // HD):
        cols = slice(head * HD, (head + 1) * HD)
        product = g_ref[:, cols].astype(jnp.float32) * o_ref[:, cols].astype(jnp.float32)
        delta_ref[head : head + 1, :] = jnp.sum(product.T, axis=0, keepdims=True)


def stats_entries(key_blocks, bits, kv_ref, q_ref, start_ref, m_ref, l_ref, bias_ref):
    heads = m_ref.shape[0]

    def step(i, carry):
        key = pick(key_blocks, i)

        @pl.when(listed(bits, key))
        def _():
            write_bias(bias_ref, start_ref, key)
            keys = kv_ref[i, 0]

            def products(head):
                return nt_dot(keys, q_ref[:, head * HD : (head + 1) * HD])

            ahead = products(0)
            for head in range(heads):
                scores = ahead * SCORE_SCALE + bias_ref[...]
                if head + 1 < heads:
                    ahead = products(head + 1)
                row = slice(head, head + 1)
                old_max = m_ref[row, :]
                new_max = jnp.maximum(old_max, jnp.max(scores, axis=0, keepdims=True))
                total = jnp.sum(jnp.exp2(scores - new_max), axis=0, keepdims=True)
                l_ref[row, :] = l_ref[row, :] * jnp.exp2(old_max - new_max) + total
                m_ref[row, :] = new_max

        return carry

    lax.fori_loop(0, len(key_blocks), step, 0)


def stats_own_kernel(q_ref, start_ref, kv0, m_ref, l_ref, bias_ref, kv_ref):
    m_ref[...] = jnp.full_like(m_ref, EMPTY)
    l_ref[...] = jnp.zeros_like(l_ref)
    kv_ref[0] = kv0[1]
    kv_ref[1] = kv0[0]
    keys = [key_block(0, 0), key_block(0, 1)]
    stats_entries(keys, listed_bits(start_ref), kv_ref, q_ref, start_ref, m_ref, l_ref, bias_ref)


def stats_mid_kernel(q_ref, start_ref, m_in, l_in, kv12, m_ref, l_ref, bias_ref, kv_ref):
    m_ref[...] = m_in[...]
    l_ref[...] = l_in[...]
    for i in range(4):
        kv_ref[i] = kv12[1 - i % 2, i // 2]
    keys = [key_block(1, i) for i in range(4)]
    stats_entries(keys, listed_bits(start_ref), kv_ref, q_ref, start_ref, m_ref, l_ref, bias_ref)


def grad_entries(key_blocks, bits, kv_ref, q_ref, g_ref, start_ref, lse_ref, delta_ref, dq_ref, bias_ref, part_ref):
    heads = lse_ref.shape[0]
    def step(i, carry):
        key = pick(key_blocks, i)
        present = listed(bits, key)

        @pl.when(jnp.logical_not(present))
        def _():
            part_ref[i] = jnp.zeros(part_ref.shape[1:], part_ref.dtype)

        @pl.when(present)
        def _():
            write_bias(bias_ref, start_ref, key)
            keys = kv_ref[i, 0]
            values = kv_ref[i, 1]
            keys_t = keys.T

            def q_head(head):
                return q_ref[:, head * HD : (head + 1) * HD]

            def g_head(head):
                return g_ref[:, head * HD : (head + 1) * HD]

            def products(head):
                return nt_dot(keys, q_head(head)), nt_dot(values, g_head(head))

            def weights(head, ahead):
                row = slice(head, head + 1)
                probs = jnp.exp2(ahead[0] * SCORE_SCALE + bias_ref[...] - lse_ref[row, :])
                d_score = probs * (ahead[1] - delta_ref[row, :])
                return probs.astype(jnp.bfloat16), d_score.astype(jnp.bfloat16)

            def sums(head, pair, acc):
                at = head * HD
                dq_ref[at : at + HD, :] += nn_dot(keys_t, pair[1])
                d_key = nn_dot(pair[1], q_head(head))
                d_value = nn_dot(pair[0], g_head(head))
                return (d_key, d_value) if acc is None else (acc[0] + d_key, acc[1] + d_value)

            acc = None
            ahead, pair = products(0), None
            for head in range(heads):
                following = products(head + 1) if head + 1 < heads else None
                if pair is not None:
                    acc = sums(head - 1, pair, acc)
                pair, ahead = weights(head, ahead), following
            acc = sums(heads - 1, pair, acc)
            part_ref[i, :, 0:HD] = acc[0] * FACTOR
            part_ref[i, :, HD:] = acc[1]

        return carry

    lax.fori_loop(0, len(key_blocks), step, 0)


def grad_far_kernel(q_ref, g_ref, start_ref, delta_ref, m_in, l_in, kv0, kv3, kv4,
                    p3_own, p_other, p4_ref, dq_ref, lse_ref, m_ref, l_ref, bias_ref, kv_ref, part_ref):
    core = core_parity()
    bits = listed_bits(start_ref)
    m_ref[...] = m_in[...]
    l_ref[...] = l_in[...]
    kv_ref[0] = kv3[1]
    kv_ref[1] = kv3[0]
    kv_ref[2] = kv4[...]
    kv_ref[3] = kv0[0]
    far = [key_block(3, 0), key_block(3, 1), key_block(3, 2)]
    stats_entries(far, bits, kv_ref, q_ref, start_ref, m_ref, l_ref, bias_ref)
    lse_ref[...] = m_ref[...] + jnp.log2(l_ref[...])
    dq_ref[...] = jnp.zeros_like(dq_ref)
    bits = jnp.where(core == 1, bits, bits & -2)
    keys = far + [key_block(0, 1)]
    grad_entries(keys, bits, kv_ref, q_ref, g_ref, start_ref, lse_ref, delta_ref, dq_ref, bias_ref, part_ref)
    p3_own[...] = part_ref[1 - core]
    p_other[0] = part_ref[core].astype(p_other.dtype)
    p_other[1] = part_ref[3].astype(p_other.dtype)
    p4_ref[...] = part_ref[2].astype(p4_ref.dtype)


def grad_mid_kernel(q_ref, g_ref, start_ref, delta_ref, lse_ref, kv12, dq_in,
                    p2_own, p_other, dq_ref, bias_ref, kv_ref, part_ref):
    del dq_in
    core = core_parity()
    kv_ref[0] = kv12[1, 1]
    kv_ref[1] = kv12[0, 1]
    kv_ref[2] = kv12[1 - core, 0]
    keys = [key_block(2, 0), key_block(2, 1), key_block(1, core)]
    bits = listed_bits(start_ref)
    grad_entries(keys, bits, kv_ref, q_ref, g_ref, start_ref, lse_ref, delta_ref, dq_ref, bias_ref, part_ref)
    p2_own[...] = part_ref[1 - core]
    p_other[0] = part_ref[2].astype(p_other.dtype)
    p_other[1] = part_ref[core].astype(p_other.dtype)


def grad_near_kernel(q_ref, g_ref, start_ref, delta_ref, lse_ref, kv_in, gathered_ref, dq_in,
                     p1_ref, dq_ref, bias_ref, kv_ref, part_ref):
    del dq_in
    core = core_parity()
    kv_ref[0] = kv_in[...]
    keys = [key_block(1, 1 - core)]
    bits = listed_bits(start_ref)
    grad_entries(keys, bits, kv_ref, q_ref, g_ref, start_ref, lse_ref, delta_ref, dq_ref, bias_ref, part_ref)
    p1_ref[...] = (part_ref[0] + gathered_ref[1 - core, 0].astype(jnp.float32)).astype(p1_ref.dtype)


def grad_own_kernel(q_ref, g_ref, start_ref, delta_ref, lse_ref, kv_in, dq_in,
                    p_own, out_ref, bias_ref, kv_ref, part_ref, dq_ref):
    kv_ref[0] = kv_in[...]
    dq_ref[...] = dq_in[...]
    keys = [lax.axis_index("cp")]
    bits = listed_bits(start_ref)
    grad_entries(keys, bits, kv_ref, q_ref, g_ref, start_ref, lse_ref, delta_ref, dq_ref, bias_ref, part_ref)
    p_own[...] = part_ref[0]
    for head in range(lse_ref.shape[0]):
        at = slice(head * HD, (head + 1) * HD)
        out_ref[:, at] = (dq_ref[at, :] * FACTOR).T.astype(out_ref.dtype)


def merge_far_kernel(own_ref, gathered_ref, out_ref):
    total = own_ref[...] + gathered_ref[1 - core_parity(), 0].astype(jnp.float32)
    out_ref[...] = total.astype(out_ref.dtype)


def merge_mid_kernel(own_ref, gathered_ref, back3_ref, back4_ref, p2_ref):
    total = own_ref[...] + gathered_ref[1 - core_parity(), 1].astype(jnp.float32)
    total += back3_ref[...].astype(jnp.float32) + back4_ref[...].astype(jnp.float32)
    p2_ref[...] = total.astype(p2_ref.dtype)


def final_kernel(own_ref, gathered_ref, back1_ref, dk_ref, dv_ref):
    total = own_ref[...] + gathered_ref[1 - core_parity(), 1].astype(jnp.float32)
    total += back1_ref[...].astype(jnp.float32)
    dk_ref[...] = total[:, 0:HD].astype(dk_ref.dtype)
    dv_ref[...] = total[:, HD:].astype(dv_ref.dtype)


def call(kernel, outs, scratch, units, *args, smem_args=0, aliases=None):
    pair = 2 * 8 * 256 * 256
    moved = sum(a.size * a.dtype.itemsize for a in args) + sum(o.size * o.dtype.itemsize for o in outs)
    spaces = [pltpu.SMEM] * smem_args + [pltpu.VMEM] * (len(args) - smem_args)
    return pl.pallas_call(
        kernel,
        out_shape=outs,
        in_specs=[pl.BlockSpec(memory_space=space) for space in spaces],
        out_specs=[pl.BlockSpec(memory_space=pltpu.VMEM) for _ in outs],
        scratch_shapes=scratch,
        input_output_aliases=aliases or {},
        compiler_params=pltpu.CompilerParams(vmem_limit_bytes=VMEM_BYTES),
        cost_estimate=pl.CostEstimate(flops=units * pair * HD, bytes_accessed=moved, transcendentals=pair),
    )(*args)


def on_device(queries, keys, values, outputs, out_grad, doc_lengths, block_offsets):
    rows, width = queries.shape
    heads = width // HD
    struct = jax.ShapeDtypeStruct
    f32, bf16 = jnp.float32, jnp.bfloat16
    stat = struct((heads, rows), f32)
    piece16, piece32 = struct((rows, 2 * HD), bf16), struct((rows, 2 * HD), f32)
    dq_part = struct((width, rows), f32)
    bias = pltpu.VMEM((rows, rows), f32)
    row_stat = pltpu.VMEM((heads, rows), f32)

    def stack(count):
        return pltpu.VMEM((count, 2, rows, HD), bf16)

    def parts(count):
        return pltpu.VMEM((count, rows, 2 * HD), f32)

    which = lax.broadcasted_iota(jnp.int32, (2, rows, HD), 0)
    kv = jnp.where(which == 0, keys[None], values[None])
    kv = lax.optimization_barrier(kv)
    kv2 = shift(kv, 4)
    both0 = gather_pair(kv)
    start, delta = call(
        prep_kernel, [struct((8, rows), jnp.int32), stat], [], 1, doc_lengths, block_offsets, out_grad, outputs,
        smem_args=1)
    m, l = call(
        stats_own_kernel, [stat, stat], [bias, stack(2)], 2, queries, start, both0)
    kv, m, l, delta = lax.optimization_barrier((kv, m, l, delta))
    kv1 = shift(kv, 2)
    kv2, m, l, delta = lax.optimization_barrier((kv2, m, l, delta))
    kv3 = shift(kv2, 2)
    kv4 = shift(kv2, 3, 1)
    both12 = gather_pair(jnp.stack([kv1, kv2]))
    m, l = call(
        stats_mid_kernel, [stat, stat], [bias, stack(4)], 4, queries, start, m, l, both12)
    both3 = gather_pair(kv3)

    known = (queries, out_grad, start, delta)
    pair16 = struct((2, rows, 2 * HD), bf16)
    p3_own, far_other, p4, dq, lse = call(
        grad_far_kernel, [piece32, pair16, piece16, dq_part, stat], [row_stat, row_stat, bias, stack(4), parts(4)],
        20, *known, m, l, both0, both3, kv4)
    back4 = shift(p4, -3, 0)
    far_both = gather_pair(far_other)
    (p3,) = call(merge_far_kernel, [piece16], [], 0, p3_own, far_both)
    back3 = shift(p3, -2)
    p2_own, mid_other, dq = call(
        grad_mid_kernel, [piece32, pair16, dq_part], [bias, stack(3), parts(3)], 15,
        *known, lse, both12, dq, aliases={6: 2})
    mid_both = gather_pair(mid_other)
    (p2,) = call(merge_mid_kernel, [piece16], [], 0, p2_own, mid_both, back3, back4)
    back2 = shift(p2, -4)
    p1, dq = call(
        grad_near_kernel, [piece16, dq_part], [bias, stack(1), parts(1)], 5,
        *known, lse, kv1, mid_both, dq, aliases={7: 1})
    back1 = shift(p1, -2)
    p0_own, grad_queries = call(
        grad_own_kernel, [piece32, struct((rows, width), bf16)],
        [bias, stack(1), parts(1), pltpu.VMEM((width, rows), f32)], 5, *known, lse, kv, dq)
    piece = struct((rows, HD), bf16)
    grad_keys, grad_values = call(final_kernel, [piece, piece], [], 0, p0_own + back2.astype(f32), far_both, back1)
    return grad_queries, grad_keys, grad_values


def solution(mesh):
    tokens = P(("dp", "cp"), "hd")
    return jax.shard_map(
        on_device,
        mesh=mesh,
        in_specs=(tokens, tokens, tokens, tokens, tokens, P("dp"), P(("dp", "cp"), None)),
        out_specs=(tokens, tokens, tokens),
        check_vma=False,
    )
```

```python
import jax
import jax.numpy as jnp
from jax import lax
from jax.experimental import pallas as pl
from jax.experimental.pallas import tpu as pltpu
from jax.sharding import PartitionSpec as P

HD = 128
FACTOR = HD ** (-0.5)
SCORE_SCALE = FACTOR * 1.4426950408889634
MASKED = -1e30
EMPTY = -1e20
VMEM_BYTES = 32 * 1024 * 1024


def shift(array, by, parity=None):
    n = lax.axis_size("cp")
    pairs = [(i, i + by) for i in range(n) if 0 <= i + by < n and parity in (None, i % 2)]
    return lax.ppermute(array, "cp", pairs)


def gather_pair(array):
    n = lax.axis_size("cp")
    return lax.all_gather(array, "cp", axis_index_groups=[[i, i + 1] for i in range(0, n, 2)])


def nt_dot(a, b):
    return lax.dot_general(a, b, (((1,), (1,)), ((), ())), preferred_element_type=jnp.float32)


def nn_dot(a, b):
    return lax.dot_general(a, b, (((1,), (0,)), ((), ())), preferred_element_type=jnp.float32)


def core_parity():
    return lax.rem(lax.axis_index("cp"), 2)


def key_block(slot, entry):
    return lax.axis_index("cp") - core_parity() + 1 - 2 * slot - entry


def listed_bits(start_ref):
    return start_ref[1, 0]


def pick(values, i):
    chosen = values[0]
    for j in range(1, len(values)):
        chosen = jnp.where(i == j, values[j], chosen)
    return chosen


def listed(bits, key):
    block = lax.axis_index("cp")
    bit = lax.shift_right_logical(bits, jnp.maximum(block - key, 0)) & 1
    return (bit == 1) & (block >= key) & (key >= 0)


def write_bias(bias_ref, start_ref, key):
    rows = bias_ref.shape[0]
    key_pos = key * rows + lax.broadcasted_iota(jnp.int32, bias_ref.shape, 0)
    q_pos = lax.axis_index("cp") * rows + lax.broadcasted_iota(jnp.int32, bias_ref.shape, 1)
    allowed = (key_pos >= start_ref[0:1, :]) & (key_pos <= q_pos)
    bias_ref[...] = jnp.where(allowed, 0.0, MASKED)


def prep_kernel(doc_ref, off_ref, g_ref, o_ref, start_ref, delta_ref):
    rows, width = g_ref.shape
    positions = lax.axis_index("cp") * rows + lax.broadcasted_iota(jnp.int32, (8, rows), 1)

    def step(doc, carry):
        end, first = carry
        end = end + doc_ref[doc]
        return (end, jnp.where(end <= positions, end, first))

    _, first = lax.fori_loop(0, doc_ref.shape[0], step, (jnp.int32(0), jnp.zeros((8, rows), jnp.int32)),
                             unroll=True)
    offsets = off_ref[...]
    listed_once = jnp.where(offsets >= 0, lax.shift_left(jnp.ones_like(offsets), jnp.maximum(offsets, 0)), 0)
    bits = jnp.sum(listed_once.astype(jnp.float32)).astype(jnp.int32)
    line = lax.broadcasted_iota(jnp.int32, first.shape, 0)
    start_ref[...] = jnp.where(line == 1, bits, first)
    ones = jnp.ones((16, HD), jnp.bfloat16)
    for head in range(width // HD):
        cols = slice(head * HD, (head + 1) * HD)
        product = g_ref[:, cols].astype(jnp.float32) * o_ref[:, cols].astype(jnp.float32)
        high = product.astype(jnp.bfloat16)
        low = (product - high.astype(jnp.float32)).astype(jnp.bfloat16)
        delta_ref[head : head + 1, :] = (nt_dot(ones, high) + nt_dot(ones, low))[0:1, :]


def stats_entries(key_blocks, bits, kv_ref, q_ref, start_ref, m_ref, l_ref, bias_ref):
    heads = m_ref.shape[0]

    def step(i, carry):
        key = pick(key_blocks, i)

        @pl.when(listed(bits, key))
        def _():
            write_bias(bias_ref, start_ref, key)
            keys = kv_ref[i, 0]

            def products(head):
                return nt_dot(keys, q_ref[:, head * HD : (head + 1) * HD])

            ahead = products(0)
            for head in range(heads):
                scores = ahead * SCORE_SCALE + bias_ref[...]
                if head + 1 < heads:
                    ahead = products(head + 1)
                row = slice(head, head + 1)
                old_max = m_ref[row, :]
                new_max = jnp.maximum(old_max, jnp.max(scores, axis=0, keepdims=True))
                total = jnp.sum(jnp.exp2(scores - new_max), axis=0, keepdims=True)
                l_ref[row, :] = l_ref[row, :] * jnp.exp2(old_max - new_max) + total
                m_ref[row, :] = new_max

        return carry

    lax.fori_loop(0, len(key_blocks), step, 0)


def stats_own_kernel(q_ref, start_ref, kv0, m_ref, l_ref, bias_ref, kv_ref):
    m_ref[...] = jnp.full_like(m_ref, EMPTY)
    l_ref[...] = jnp.zeros_like(l_ref)
    kv_ref[0] = kv0[1]
    kv_ref[1] = kv0[0]
    keys = [key_block(0, 0), key_block(0, 1)]
    stats_entries(keys, listed_bits(start_ref), kv_ref, q_ref, start_ref, m_ref, l_ref, bias_ref)


def stats_mid_kernel(q_ref, start_ref, m_in, l_in, kv12, m_ref, l_ref, bias_ref, kv_ref):
    m_ref[...] = m_in[...]
    l_ref[...] = l_in[...]
    for i in range(4):
        kv_ref[i] = kv12[1 - i % 2, i // 2]
    keys = [key_block(1, i) for i in range(4)]
    stats_entries(keys, listed_bits(start_ref), kv_ref, q_ref, start_ref, m_ref, l_ref, bias_ref)


def grad_entries(key_blocks, bits, kv_ref, q_ref, g_ref, start_ref, lse_ref, delta_ref, dq_ref, bias_ref, part_ref):
    heads = lse_ref.shape[0]
    def step(i, carry):
        key = pick(key_blocks, i)
        present = listed(bits, key)

        @pl.when(jnp.logical_not(present))
        def _():
            part_ref[i] = jnp.zeros(part_ref.shape[1:], part_ref.dtype)

        @pl.when(present)
        def _():
            write_bias(bias_ref, start_ref, key)
            keys = kv_ref[i, 0]
            values = kv_ref[i, 1]
            keys_t = keys.T

            def q_head(head):
                return q_ref[:, head * HD : (head + 1) * HD]

            def g_head(head):
                return g_ref[:, head * HD : (head + 1) * HD]

            def products(head):
                return nt_dot(keys, q_head(head)), nt_dot(values, g_head(head))

            def weights(head, ahead):
                row = slice(head, head + 1)
                probs = jnp.exp2(ahead[0] * SCORE_SCALE + bias_ref[...] - lse_ref[row, :])
                d_score = probs * (ahead[1] - delta_ref[row, :])
                return probs.astype(jnp.bfloat16), d_score.astype(jnp.bfloat16)

            def sums(head, pair, acc):
                at = head * HD
                dq_ref[at : at + HD, :] += nn_dot(keys_t, pair[1])
                d_key = nn_dot(pair[1], q_head(head))
                d_value = nn_dot(pair[0], g_head(head))
                return (d_key, d_value) if acc is None else (acc[0] + d_key, acc[1] + d_value)

            acc = None
            ahead, pair = products(0), None
            for head in range(heads):
                following = products(head + 1) if head + 1 < heads else None
                if pair is not None:
                    acc = sums(head - 1, pair, acc)
                pair, ahead = weights(head, ahead), following
            acc = sums(heads - 1, pair, acc)
            part_ref[i, :, 0:HD] = acc[0] * FACTOR
            part_ref[i, :, HD:] = acc[1]

        return carry

    lax.fori_loop(0, len(key_blocks), step, 0)


def grad_far_kernel(q_ref, g_ref, start_ref, delta_ref, m_in, l_in, kv0, kv3, kv4,
                    p3_own, p_other, p4_ref, dq_ref, lse_ref, m_ref, l_ref, bias_ref, kv_ref, part_ref):
    core = core_parity()
    bits = listed_bits(start_ref)
    m_ref[...] = m_in[...]
    l_ref[...] = l_in[...]
    kv_ref[0] = kv3[1]
    kv_ref[1] = kv3[0]
    kv_ref[2] = kv4[...]
    kv_ref[3] = kv0[0]
    far = [key_block(3, 0), key_block(3, 1), key_block(3, 2)]
    stats_entries(far, bits, kv_ref, q_ref, start_ref, m_ref, l_ref, bias_ref)
    lse_ref[...] = m_ref[...] + jnp.log2(l_ref[...])
    dq_ref[...] = jnp.zeros_like(dq_ref)
    bits = jnp.where(core == 1, bits, bits & -2)
    keys = far + [key_block(0, 1)]
    grad_entries(keys, bits, kv_ref, q_ref, g_ref, start_ref, lse_ref, delta_ref, dq_ref, bias_ref, part_ref)
    p3_own[...] = part_ref[1 - core]
    p_other[0] = part_ref[core].astype(p_other.dtype)
    p_other[1] = part_ref[3].astype(p_other.dtype)
    p4_ref[...] = part_ref[2].astype(p4_ref.dtype)


def grad_mid_kernel(q_ref, g_ref, start_ref, delta_ref, lse_ref, kv12, dq_in,
                    p2_own, p_other, dq_ref, bias_ref, kv_ref, part_ref):
    del dq_in
    core = core_parity()
    kv_ref[0] = kv12[1, 1]
    kv_ref[1] = kv12[0, 1]
    kv_ref[2] = kv12[1 - core, 0]
    keys = [key_block(2, 0), key_block(2, 1), key_block(1, core)]
    bits = listed_bits(start_ref)
    grad_entries(keys, bits, kv_ref, q_ref, g_ref, start_ref, lse_ref, delta_ref, dq_ref, bias_ref, part_ref)
    p2_own[...] = part_ref[1 - core]
    p_other[0] = part_ref[2].astype(p_other.dtype)
    p_other[1] = part_ref[core].astype(p_other.dtype)


def grad_near_kernel(q_ref, g_ref, start_ref, delta_ref, lse_ref, kv_in, gathered_ref, dq_in,
                     p1_ref, dq_ref, bias_ref, kv_ref, part_ref):
    del dq_in
    core = core_parity()
    kv_ref[0] = kv_in[...]
    keys = [key_block(1, 1 - core)]
    bits = listed_bits(start_ref)
    grad_entries(keys, bits, kv_ref, q_ref, g_ref, start_ref, lse_ref, delta_ref, dq_ref, bias_ref, part_ref)
    p1_ref[...] = (part_ref[0] + gathered_ref[1 - core, 0].astype(jnp.float32)).astype(p1_ref.dtype)


def grad_own_kernel(q_ref, g_ref, start_ref, delta_ref, lse_ref, kv_in, dq_in,
                    p_own, out_ref, bias_ref, kv_ref, part_ref, dq_ref):
    kv_ref[0] = kv_in[...]
    dq_ref[...] = dq_in[...]
    keys = [lax.axis_index("cp")]
    bits = listed_bits(start_ref)
    grad_entries(keys, bits, kv_ref, q_ref, g_ref, start_ref, lse_ref, delta_ref, dq_ref, bias_ref, part_ref)
    p_own[...] = part_ref[0]
    for head in range(lse_ref.shape[0]):
        at = slice(head * HD, (head + 1) * HD)
        out_ref[:, at] = (dq_ref[at, :] * FACTOR).T.astype(out_ref.dtype)


def merge_far_kernel(own_ref, gathered_ref, out_ref):
    total = own_ref[...] + gathered_ref[1 - core_parity(), 0].astype(jnp.float32)
    out_ref[...] = total.astype(out_ref.dtype)


def merge_mid_kernel(own_ref, gathered_ref, back3_ref, back4_ref, p2_ref):
    total = own_ref[...] + gathered_ref[1 - core_parity(), 1].astype(jnp.float32)
    total += back3_ref[...].astype(jnp.float32) + back4_ref[...].astype(jnp.float32)
    p2_ref[...] = total.astype(p2_ref.dtype)


def final_kernel(own_ref, gathered_ref, back1_ref, dk_ref, dv_ref):
    total = own_ref[...] + gathered_ref[1 - core_parity(), 1].astype(jnp.float32)
    total += back1_ref[...].astype(jnp.float32)
    dk_ref[...] = total[:, 0:HD].astype(dk_ref.dtype)
    dv_ref[...] = total[:, HD:].astype(dv_ref.dtype)


def call(kernel, outs, scratch, units, *args, smem_args=0, aliases=None):
    pair = 2 * 8 * 256 * 256
    moved = sum(a.size * a.dtype.itemsize for a in args) + sum(o.size * o.dtype.itemsize for o in outs)
    spaces = [pltpu.SMEM] * smem_args + [pltpu.VMEM] * (len(args) - smem_args)
    return pl.pallas_call(
        kernel,
        out_shape=outs,
        in_specs=[pl.BlockSpec(memory_space=space) for space in spaces],
        out_specs=[pl.BlockSpec(memory_space=pltpu.VMEM) for _ in outs],
        scratch_shapes=scratch,
        input_output_aliases=aliases or {},
        compiler_params=pltpu.CompilerParams(vmem_limit_bytes=VMEM_BYTES),
        cost_estimate=pl.CostEstimate(flops=units * pair * HD, bytes_accessed=moved, transcendentals=pair),
    )(*args)


def on_device(queries, keys, values, outputs, out_grad, doc_lengths, block_offsets):
    rows, width = queries.shape
    heads = width // HD
    struct = jax.ShapeDtypeStruct
    f32, bf16 = jnp.float32, jnp.bfloat16
    stat = struct((heads, rows), f32)
    piece16, piece32 = struct((rows, 2 * HD), bf16), struct((rows, 2 * HD), f32)
    dq_part = struct((width, rows), f32)
    bias = pltpu.VMEM((rows, rows), f32)
    row_stat = pltpu.VMEM((heads, rows), f32)

    def stack(count):
        return pltpu.VMEM((count, 2, rows, HD), bf16)

    def parts(count):
        return pltpu.VMEM((count, rows, 2 * HD), f32)

    which = lax.broadcasted_iota(jnp.int32, (2, rows, HD), 0)
    kv = jnp.where(which == 0, keys[None], values[None])
    kv = lax.optimization_barrier(kv)
    kv2 = shift(kv, 4)
    both0 = gather_pair(kv)
    start, delta = call(
        prep_kernel, [struct((8, rows), jnp.int32), stat], [], 1, doc_lengths, block_offsets, out_grad, outputs,
        smem_args=1)
    m, l = call(
        stats_own_kernel, [stat, stat], [bias, stack(2)], 2, queries, start, both0)
    kv, m, l, delta = lax.optimization_barrier((kv, m, l, delta))
    kv1 = shift(kv, 2)
    kv2, m, l, delta = lax.optimization_barrier((kv2, m, l, delta))
    kv3 = shift(kv2, 2)
    kv4 = shift(kv2, 3, 1)
    both12 = gather_pair(jnp.stack([kv1, kv2]))
    m, l = call(
        stats_mid_kernel, [stat, stat], [bias, stack(4)], 4, queries, start, m, l, both12)
    both3 = gather_pair(kv3)

    known = (queries, out_grad, start, delta)
    pair16 = struct((2, rows, 2 * HD), bf16)
    p3_own, far_other, p4, dq, lse = call(
        grad_far_kernel, [piece32, pair16, piece16, dq_part, stat], [row_stat, row_stat, bias, stack(4), parts(4)],
        20, *known, m, l, both0, both3, kv4)
    back4 = shift(p4, -3, 0)
    far_both = gather_pair(far_other)
    (p3,) = call(merge_far_kernel, [piece16], [], 0, p3_own, far_both)
    back3 = shift(p3, -2)
    p2_own, mid_other, dq = call(
        grad_mid_kernel, [piece32, pair16, dq_part], [bias, stack(3), parts(3)], 15,
        *known, lse, both12, dq, aliases={6: 2})
    mid_both = gather_pair(mid_other)
    (p2,) = call(merge_mid_kernel, [piece16], [], 0, p2_own, mid_both, back3, back4)
    back2 = shift(p2, -4)
    p1, dq = call(
        grad_near_kernel, [piece16, dq_part], [bias, stack(1), parts(1)], 5,
        *known, lse, kv1, mid_both, dq, aliases={7: 1})
    back1 = shift(p1, -2)
    p0_own, grad_queries = call(
        grad_own_kernel, [piece32, struct((rows, width), bf16)],
        [bias, stack(1), parts(1), pltpu.VMEM((width, rows), f32)], 5, *known, lse, kv, dq)
    piece = struct((rows, HD), bf16)
    grad_keys, grad_values = call(final_kernel, [piece, piece], [], 0, p0_own + back2.astype(f32), far_both, back1)
    return grad_queries, grad_keys, grad_values


def solution(mesh):
    tokens = P(("dp", "cp"), "hd")
    return jax.shard_map(
        on_device,
        mesh=mesh,
        in_specs=(tokens, tokens, tokens, tokens, tokens, P("dp"), P(("dp", "cp"), None)),
        out_specs=(tokens, tokens, tokens),
        check_vma=False,
    )
```
